256 devices in a mesh: dp: 8 (over x, core), expert: 32 (over y, z).
Axes of the slice: x: 4, y: 4, z: 8, core: 2. Of those that a mesh axis runs over, the one named last changes fastest.
Arguments:
- tokens: bfloat16 [512, 7168], P('expert'), may hold values from -6 to 6
- out_grad: bfloat16 [512, 7168], P('expert'), may hold values from -6 to 6
- expert_ids: int32 [512, 8], P('expert'), may hold values from 0 to 31, all different within a row; in each aligned block of 16 rows (0 to 15, 16 to 31, ...) at most 6 rows name the same one
- gate_weights: float32 [512, 8], P('expert'), may hold values from 0.05 to 0.3
- base_gate: bfloat16 [32, 7168, 2048], P('expert', None, 'dp'), may hold values from -0.0625 to 0.0625
- base_up: bfloat16 [32, 7168, 2048], P('expert', None, 'dp'), may hold values from -0.0625 to 0.0625
- base_down: bfloat16 [32, 2048, 7168], P('expert', 'dp'), may hold values from -0.125 to 0.125
- block_ids: int32 [32, 16, 2], P('expert', 'dp'), may hold values from 0 to 167, as said below
- delta: float32 [32, 16, 2, 128, 128], P('expert', 'dp'), may hold values from -4 to 4
- moment_one: float32 [32, 16, 2, 128, 128], P('expert', 'dp'), may hold values from -0.24 to 0.24
- moment_two: float32 [32, 16, 2, 128, 128], P('expert', 'dp'), may hold values from 0.0005 to 0.005
Outputs:
- in_grad: bfloat16 [512, 7168], P('expert', 'dp')
- new_delta: float32 [32, 16, 2, 128, 128], P('expert', 'dp')
The draws below stay inside these ranges and needn't reach their ends.
Inputs may be any that keep to these rules, and one draw needn't show every extreme that they name: `expert_ids`: each token names 8 different experts, and among the 16 tokens of one index of expert no expert is named more than 6 times. `block_ids`: the 2 ids of one column of blocks of one expert are different.
All inputs are finite; a program needn't handle non-finite values.
Results may differ from the reference program's by a relative error of at most 0.019.
Values may be sent and summed in bfloat16 or wider, within the bound.
A program may use at most 128 MiB of HBM per device.

```python
import math
from functools import partial
import jax
import jax.numpy as jnp
import numpy as np
from jax import lax

D = 7168
FF = 2048
EXPERTS = 32
TOP = 8
BLK = 128
NBLK = 2
TOK_DEV = 16
CAP = 6
TOKENS = 512
N_DP = 8
N_EXPERT = 32


def draw_block_ids(key, part):
    key = jax.random.fold_in(key, 7)
    choices_all = 3 * (D // BLK)
    count = EXPERTS * (FF // BLK)
    keys = jax.random.split(key, count)

    def one_row(row_key):
        return jax.random.permutation(row_key, choices_all)[:NBLK].astype(jnp.int32)
    picked = jax.vmap(one_row)(keys)
    first_row = jnp.remainder(picked[0] + (choices_all - 1 - picked[0, 0]), choices_all)
    second_row = jnp.remainder(picked[1] - picked[1, 0], choices_all)
    picked = picked.at[0].set(first_row).at[1].set(second_row)
    return picked.reshape(EXPERTS, FF // BLK, NBLK).astype(jnp.int32)


def shard_levels(stream_key, extent, pieces, low, top_value):
    level = 1.0
    for position, shards_of in pieces:
        draws = jax.random.uniform(jax.random.fold_in(jax.random.fold_in(stream_key, 6), position), (shards_of,), jnp.float32, low / len(pieces), top_value / len(pieces))
        level = level * jnp.repeat(jnp.exp(draws), extent[position] // shards_of).reshape((-1,) + (1,) * (len(extent) - 1 - position))
    return level


def deal_out(stream_key, own, number, rows, number_of, top, most, skew):
    ranking = jax.random.permutation(stream_key, number_of)
    heavy_load, common = load_shares(number_of, rows * top, most, skew, True), load_shares(number_of, rows * top, most, skew, False)
    places = jnp.arange(number_of)

    def named(sizes, rotation):
        used = int((sizes > 0).sum())
        fixed = max(1, used // 4)
        passed = fixed + (places - fixed + rotation * (used - fixed)) % max(1, number_of - fixed)
        return jnp.zeros((number_of,), jnp.int32).at[ranking[jnp.where(places < fixed, places, passed)]].set(jnp.asarray(sizes, jnp.int32))

    sizes = jnp.where(number % 4 == 0, named(heavy_load, number // 4), named(common, number - number // 4 - 1))
    mixed = jax.random.permutation(jax.random.fold_in(own, 3), number_of)
    donor, receiver = mixed[0:number_of // 2 * 2:2], mixed[1:number_of // 2 * 2:2]
    room = jnp.minimum(sizes[donor] - 1, most - sizes[receiver]) // 2
    room = jnp.where((donor == ranking[0]) | (receiver == ranking[0]) | (sizes[receiver] == 0), 0, jnp.maximum(room, 0))
    passed = jax.random.randint(jax.random.fold_in(own, 4), (number_of // 2,), 0, 1 << 20) % (room + 1)
    sizes = sizes.at[donor].add(-passed).at[receiver].add(passed)
    items = jnp.searchsorted(jnp.cumsum(sizes), jnp.arange(rows * top), side="right").astype(jnp.int32)
    listing = items.reshape(top, rows).T
    listing = listing[jax.random.permutation(jax.random.fold_in(own, 1), rows)]
    rotation = jax.random.randint(jax.random.fold_in(own, 2), (rows, 1), 0, top)
    return jnp.take_along_axis(listing, (jnp.arange(top)[None, :] + rotation) % top, axis=1)


def load_shares(amount, total, bound, lean, full):
    weights = [(1 << 20) // math.isqrt(grade ** lean) + 1 for grade in range(1, amount + 1)]
    largest = bound if full else min(bound, max(-(-total // amount), total * weights[0] // sum(weights)))
    least = 1 if total - largest >= amount - 1 else 0
    holding, spare = [largest] + [least] * (amount - 1), total - largest - least * (amount - 1)
    while spare > 0:
        candidates = [i for i in range(1, amount) if holding[i] < largest] or [i for i in range(1, amount) if holding[i] < bound]
        whole, budget = sum([weights[i] for i in candidates]), spare
        for i in candidates:
            more = min(bound - holding[i], max(1, budget * weights[i] // whole), spare)
            holding[i] = holding[i] + more
            spare = spare - more
    return np.array(holding)


def noise(stream_key, shape, spread, most, shards=(), kind=jnp.bfloat16):
    array = jax.random.normal(stream_key, shape, jnp.float32) * spread
    if len(shards) > 0:
        array = shard_levels(stream_key, shape, shards, -0.22, 0.18) * array
    return jnp.clip(array, min=-most, max=most).astype(kind)


def setup_inputs(seed: int = 0) -> dict:
    arg_keys = jax.random.split(jax.random.key(seed), 12)
    tokens = noise(arg_keys[0], (TOKENS, D), 1.0, 6.0, ((0, 32),))
    out_grad = noise(arg_keys[1], (TOKENS, D), 1.0, 6.0, ((0, 32),))
    expert_ids_keys = jax.random.split(jax.random.fold_in(arg_keys[2], 1), TOKENS // TOK_DEV)
    expert_ids_turns = jax.random.permutation(jax.random.fold_in(arg_keys[2], 3), TOKENS // TOK_DEV)
    expert_ids = jax.vmap(lambda own, number: deal_out(jax.random.fold_in(arg_keys[2], 2), own, number, TOK_DEV, EXPERTS, TOP, CAP, 2))(expert_ids_keys, expert_ids_turns).reshape((TOKENS, TOP))
    gate_weights = jnp.clip(0.05 + 0.25 * jax.random.uniform(arg_keys[3], (TOKENS, TOP), jnp.float32) ** shard_levels(arg_keys[3], (TOKENS, TOP), ((0, 32),), -0.2, 0.2), 0.05, 0.3)
    base_gate = noise(arg_keys[4], (EXPERTS, D, FF), D ** -0.5, 0.0625, ((0, 32), (2, 8)))
    base_up = noise(arg_keys[5], (EXPERTS, D, FF), D ** -0.5, 0.0625, ((0, 32), (2, 8)))
    base_down = noise(arg_keys[6], (EXPERTS, FF, D), FF ** -0.5, 0.125, ((0, 32), (1, 8)))
    block_ids = draw_block_ids(jax.random.fold_in(arg_keys[11], 71), 0)
    delta = noise(arg_keys[8], (EXPERTS, FF // BLK, NBLK, BLK, BLK), 1.0, 4.0, ((0, 32), (1, 8)), jnp.float32)
    moment_one = noise(arg_keys[9], (EXPERTS, FF // BLK, NBLK, BLK, BLK), 0.04, 0.24, ((0, 32), (1, 8)), jnp.float32)
    moment_two = jnp.clip(jnp.exp(math.log(0.005) - 2.30258502 * jax.random.uniform(arg_keys[10], (EXPERTS, FF // BLK, NBLK, BLK, BLK), jnp.float32) ** shard_levels(arg_keys[10], (EXPERTS, FF // BLK, NBLK, BLK, BLK), ((0, 32), (1, 8)), -0.2, 0.2)), 0.0005, 0.005)
    return dict(tokens=tokens, out_grad=out_grad, expert_ids=expert_ids, gate_weights=gate_weights, base_gate=base_gate, base_up=base_up, base_down=base_down, block_ids=block_ids, delta=delta, moment_one=moment_one, moment_two=moment_two)


beta_one = 0.9
beta_two = 0.95
learn_rate = 0.5
adam_eps = 1e-08
corr_one = 1.0 - beta_one ** 10
corr_two = 1.0 - beta_two ** 10

def slot_tables(expert_ids, gate_weights, experts, capacity):
    flat_ids = expert_ids.reshape(-1)
    picked = (flat_ids[:, None] == jnp.arange(experts, dtype=jnp.int32)[None, :]).astype(jnp.int32)
    rank_of = lax.optimization_barrier(jnp.sum((jnp.cumsum(picked, axis=0) - 1) * picked, axis=1))
    slot_ids = flat_ids * capacity + rank_of
    owners = jnp.arange(flat_ids.shape[0], dtype=jnp.int32) // expert_ids.shape[1]
    token_of_slot = jnp.full((experts * capacity,), -1, jnp.int32).at[slot_ids].set(owners)
    gate_of_slot = jnp.zeros((experts * capacity,), jnp.float32).at[slot_ids].set(gate_weights.reshape(-1).astype(jnp.float32))
    return (token_of_slot, gate_of_slot)

def reference(tokens, out_grad, expert_ids, gate_weights, base_gate, base_up, base_down, block_ids, delta, moment_one, moment_two):
    src_ids = expert_ids.reshape(N_EXPERT, TOK_DEV, TOP)
    src_gates = gate_weights.reshape(N_EXPERT, TOK_DEV, TOP)
    tables = jax.vmap(partial(slot_tables, experts=EXPERTS, capacity=CAP))
    token_of_slot, gate_of_slot = tables(src_ids, src_gates)
    offsets = jnp.arange(N_EXPERT, dtype=jnp.int32)[:, None] * TOK_DEV
    global_tok = jnp.where(token_of_slot >= 0, token_of_slot + offsets, -1)
    slot_tok = global_tok.reshape(N_EXPERT, EXPERTS, CAP).transpose(1, 0, 2).reshape(EXPERTS, N_EXPERT * CAP)
    slot_gate = gate_of_slot.reshape(N_EXPERT, EXPERTS, CAP).transpose(1, 0, 2).reshape(EXPERTS, N_EXPERT * CAP)
    dim_blocks = D // BLK
    hid_blocks = FF // BLK
    block_kind = block_ids // dim_blocks
    row_block = block_ids % dim_blocks
    scales = jnp.where(block_kind == 2, FF ** (-0.5), D ** (-0.5)).astype(jnp.float32)
    columns = jnp.broadcast_to(jnp.arange(hid_blocks, dtype=jnp.int32)[:, None], (hid_blocks, NBLK))
    slice_ff = FF // N_DP

    def one_expert(in_total, inputs):
        e_gate, e_up, e_down, e_kind, e_row, e_delta, e_scale, e_tok, e_gate_val = inputs
        placed = jnp.zeros((3, dim_blocks, hid_blocks, BLK, BLK), jnp.float32)
        placed = placed.at[e_kind, e_row, columns].set(e_scale[..., None, None] * e_delta)
        add_gate = placed[0].transpose(0, 2, 1, 3).reshape(D, FF)
        add_up = placed[1].transpose(0, 2, 1, 3).reshape(D, FF)
        add_down = placed[2].transpose(1, 2, 0, 3).reshape(FF, D)
        gate_eff = (e_gate.astype(jnp.float32) + add_gate).astype(jnp.bfloat16)
        up_eff = (e_up.astype(jnp.float32) + add_up).astype(jnp.bfloat16)
        down_eff = (e_down.astype(jnp.float32) + add_down).astype(jnp.bfloat16)
        is_valid = e_tok >= 0
        safe_tok = jnp.maximum(e_tok, 0)
        rows_in = jnp.where(is_valid[:, None], tokens[safe_tok], jnp.zeros((), tokens.dtype))
        grads_in = (e_gate_val[:, None] * out_grad[safe_tok].astype(jnp.float32)).astype(jnp.bfloat16)
        gate_pre = jnp.dot(rows_in, gate_eff, preferred_element_type=jnp.float32)
        up_pre = jnp.dot(rows_in, up_eff, preferred_element_type=jnp.float32)
        sigmoid_gate = jax.nn.sigmoid(gate_pre)
        swish_gate = gate_pre * sigmoid_gate
        hidden = (swish_gate * up_pre).astype(jnp.bfloat16)
        hidden_grad = jnp.dot(grads_in, down_eff.T, preferred_element_type=jnp.float32)
        gate_grad = (hidden_grad * up_pre * sigmoid_gate * (1.0 + gate_pre * (1.0 - sigmoid_gate))).astype(jnp.bfloat16)
        up_grad = (hidden_grad * swish_gate).astype(jnp.bfloat16)
        partial_total = jnp.zeros((rows_in.shape[0], D), jnp.float32)
        for member in range(N_DP):
            low_end = member * slice_ff
            high_end = low_end + slice_ff
            piece_sum = jnp.dot(gate_grad[:, low_end:high_end], gate_eff[:, low_end:high_end].T, preferred_element_type=jnp.float32)
            piece_sum = piece_sum + jnp.dot(up_grad[:, low_end:high_end], up_eff[:, low_end:high_end].T, preferred_element_type=jnp.float32)
            rounded = lax.optimization_barrier(piece_sum.astype(jnp.bfloat16))
            partial_total = partial_total + rounded.astype(jnp.float32)
        in_total = in_total.at[safe_tok].add(jnp.where(is_valid[:, None], partial_total, 0.0))

        def block_grad(kind_now, row_now, column):
            x_part = lax.dynamic_slice_in_dim(rows_in, (row_now * BLK).astype(jnp.int32), BLK, 1)
            y_part = lax.dynamic_slice_in_dim(grads_in, (row_now * BLK).astype(jnp.int32), BLK, 1)
            h_part = lax.dynamic_slice_in_dim(hidden, (column * BLK).astype(jnp.int32), BLK, 1)
            g_part = lax.dynamic_slice_in_dim(gate_grad, (column * BLK).astype(jnp.int32), BLK, 1)
            u_part = lax.dynamic_slice_in_dim(up_grad, (column * BLK).astype(jnp.int32), BLK, 1)
            left_part = jnp.where(kind_now == 2, h_part, x_part).astype(jnp.float32)
            right_part = jnp.where(kind_now == 0, g_part, jnp.where(kind_now == 1, u_part, y_part)).astype(jnp.float32)
            return jnp.dot(left_part.T, right_part, precision=lax.Precision.HIGHEST)
        grads_here = jax.vmap(jax.vmap(block_grad))(e_kind, e_row, columns) * e_scale[..., None, None]
        return (in_total, grads_here)
    inputs = (base_gate, base_up, base_down, block_kind, row_block, delta, scales, slot_tok, slot_gate)
    in_total, block_grads = lax.scan(one_expert, jnp.zeros((TOKENS, D), jnp.float32), inputs)
    mom_one = beta_one * moment_one + (1.0 - beta_one) * block_grads
    mom_two = beta_two * moment_two + (1.0 - beta_two) * block_grads * block_grads
    new_delta = delta - learn_rate * (mom_one / corr_one) / (jnp.sqrt(mom_two / corr_two) + adam_eps)
    return (in_total.astype(jnp.bfloat16), new_delta)
```

```python
import functools

import jax
import jax.numpy as jnp
from jax import lax
from jax.experimental import pallas as pl
from jax.experimental.pallas import tpu as pltpu
from jax.sharding import PartitionSpec as P

D = 7168
FF = 2048
BLK = 128
CAP = 6
PAD = 8
TOK = 16
TOP = 8
HID = 256
ROWS = 192
HALF = ROWS // 2
FEAT = 896
FBLK = D // BLK
NT_DEV = FEAT // BLK
CHUNKS = ((0, 512), (512, 384))
NCH = len(CHUNKS)
WIDE = 256

beta_one = 0.9
beta_two = 0.95
learn_rate = 0.5
adam_eps = 1e-08
corr_one = 1.0 - beta_one**10
corr_two = 1.0 - beta_two**10

MESH = pl.DeviceIdType.MESH
F32 = jnp.float32
BF16 = jnp.bfloat16
NT = (((1,), (1,)), ((), ()))
TN = (((0,), (0,)), ((), ()))


def mm(a, b):
    return jnp.dot(a, b, preferred_element_type=F32)


def mm_nt(a, b):
    return lax.dot_general(a, b, NT, preferred_element_type=F32)


def mm_tn(a, b):
    return lax.dot_general(a, b, TN, preferred_element_type=F32)


def slot_matrix(ids_t, gates_t, count, width_bits):
    place = lax.broadcasted_iota(jnp.int32, (count, TOK), 0)
    expert = place >> width_bits
    rank = (place & (PAD - 1)).astype(F32)
    named = jnp.zeros((count, TOK), F32)
    gates = jnp.zeros((count, TOK), F32)
    for k in range(TOP):
        hit = expert == ids_t[k : k + 1, :]
        named = jnp.where(hit, 1.0, named)
        gates = jnp.where(hit, gates_t[k : k + 1, :], gates)
    earlier = (
        lax.broadcasted_iota(jnp.int32, (TOK, TOK), 0)
        < lax.broadcasted_iota(jnp.int32, (TOK, TOK), 1)
    ).astype(F32)
    before = mm(named.astype(BF16), earlier.astype(BF16))
    chosen = jnp.where(before == rank, named, 0.0)
    return chosen, gates


def kernel(
    nexp,
    ndp,
    ids_ref,
    gates_ref,
    bids,
    tok_hbm,
    og_hbm,
    wg_hbm,
    wu_hbm,
    wd_hbm,
    delta_hbm,
    m1_hbm,
    m2_hbm,
    in_grad,
    new_delta,
    tok_v,
    og_v,
    msg,
    recv,
    gath,
    wgu,
    wd,
    delta_v,
    m1_v,
    m2_v,
    dz,
    gu_acc,
    hg_acc,
    gu_b,
    hid_b,
    p_send,
    p_recv,
    far_s,
    right_s,
    left_s,
    right_t,
    left_t,
    own_t,
    far_l,
    far_r,
    from_l,
    from_r,
    msg_d,
    recv_d,
    load_sem,
    a_send,
    a_recv,
    a_loc,
    g_send,
    g_recv,
    p_ssem,
    p_rsem,
    x_ssem,
    x_rsem,
    d_send,
    d_recv,
    d_loc,
):
    me_d = lax.axis_index("dp")
    me_e = lax.axis_index("expert")
    core = lax.rem(me_d, 2)
    flip = 1 - 2 * core
    partner = me_d + flip
    right = lax.rem(me_d + 2, ndp)
    left = lax.rem(me_d + ndp - 2, ndp)
    far = lax.rem(me_d + 4, ndp)

    barrier = pltpu.get_barrier_semaphore()

    def greet(i, carry):
        pl.semaphore_signal(
            barrier, inc=1, device_id={"expert": lax.rem(me_e + i, nexp)}, device_id_type=MESH
        )
        return carry

    lax.fori_loop(1, nexp, greet, 0)
    for other in (partner, right, left):
        pl.semaphore_signal(barrier, inc=1, device_id={"dp": other}, device_id_type=MESH)

    first = pl.multiple_of(me_d * FEAT, BLK)
    loads = [
        pltpu.make_async_copy(tok_hbm.at[:, pl.ds(first, FEAT)], tok_v, load_sem.at[0]),
        pltpu.make_async_copy(og_hbm.at[:, pl.ds(first, FEAT)], og_v, load_sem.at[1]),
        pltpu.make_async_copy(delta_hbm.at[0], delta_v, load_sem.at[2]),
        pltpu.make_async_copy(wg_hbm.at[0], wgu.at[:, pl.ds(0, HID)], load_sem.at[3]),
        pltpu.make_async_copy(wu_hbm.at[0], wgu.at[:, pl.ds(HID, HID)], load_sem.at[4]),
        pltpu.make_async_copy(wd_hbm.at[0], wd, load_sem.at[5]),
        pltpu.make_async_copy(m1_hbm.at[0], m1_v, load_sem.at[6]),
        pltpu.make_async_copy(m2_hbm.at[0], m2_v, load_sem.at[7]),
    ]
    for load in loads:
        load.start()

    ids_t = ids_ref[...]
    gates_t = gates_ref[...]
    chosen, gates = slot_matrix(ids_t, gates_t, nexp * PAD, 3)
    gate_of = jnp.sum(chosen * gates, axis=1, keepdims=True)
    chosen_b = chosen.astype(BF16)
    loads[0].wait()
    loads[1].wait()
    for off, width in CHUNKS:
        cols = pl.ds(off, width)
        rows_out = mm(chosen_b, tok_v[:, cols])
        grads_out = mm(chosen_b, og_v[:, cols]) * gate_of
        msg[:, :, cols] = jnp.concatenate(
            [rows_out.reshape(nexp, PAD, width), grads_out.reshape(nexp, PAD, width)], axis=1
        ).astype(BF16)

    pl.semaphore_wait(barrier, nexp - 1 + 3)

    a_own = []
    for c, (off, width) in enumerate(CHUNKS):
        cols = pl.ds(off, width)

        def send(i, carry, c=c, cols=cols):
            to = lax.rem(me_e + i, nexp)
            pltpu.make_async_remote_copy(
                src_ref=msg.at[to, :, cols],
                dst_ref=recv.at[me_e, :, cols],
                send_sem=a_send.at[c],
                recv_sem=a_recv.at[c],
                device_id={"expert": to},
                device_id_type=MESH,
            ).start()
            return carry

        lax.fori_loop(1, nexp, send, 0)
        own = pltpu.make_async_copy(msg.at[me_e, :, cols], recv.at[me_e, :, cols], a_loc.at[c])
        own.start()
        a_own.append(own)

    loads[2].wait()
    for c in range(2):
        for m in range(2):
            scale = jnp.where(bids[0, c, m] >= 2 * FBLK, FF**-0.5, D**-0.5).astype(F32)
            dz[3 * c + m] = delta_v[c, m] * scale
        dz[3 * c + 2] = jnp.zeros((BLK, BLK), F32)
    for i in (3, 4, 5):
        loads[i].wait()

    def which(c, want):
        return 3 * c + jnp.where(bids[0, c, 0] == want, 0, jnp.where(bids[0, c, 1] == want, 1, 2))

    def adjust(j, carry):
        at = pl.ds(pl.multiple_of(j * BLK, BLK), BLK)
        for kind in range(2):
            for c in range(2):
                lanes = pl.ds(kind * HID + c * BLK, BLK)
                old = wgu[at, lanes].astype(F32)
                wgu[at, lanes] = (old + dz[which(c, kind * FBLK + j)]).astype(BF16)
        for c in range(2):
            subl = pl.ds(c * BLK, BLK)
            old = wd[subl, at].astype(F32)
            wd[subl, at] = (old + dz[which(c, 2 * FBLK + j)]).astype(BF16)
        return carry

    lax.fori_loop(0, FBLK, adjust, 0)

    gu_acc[...] = jnp.zeros_like(gu_acc)
    hg_acc[...] = jnp.zeros_like(hg_acc)

    row_i = lax.broadcasted_iota(jnp.int32, (2 * ROWS, nexp * 16), 0)
    col_i = lax.broadcasted_iota(jnp.int32, (2 * ROWS, nexp * 16), 1)
    col_r = col_i & (PAD - 1)
    want = (col_i >> 4) * CAP + col_r + jnp.where((col_i & PAD) != 0, ROWS, 0)
    compact = jnp.where((row_i == want) & (col_r < CAP), 1.0, 0.0).astype(BF16)

    def other(d):
        return d + flip

    both = pl.ds(0, 2 * ROWS)
    rows_s = pl.ds(0, ROWS)
    grads_s = pl.ds(ROWS, ROWS)

    def part(c, idx, d, which_rows, to):
        off, width = CHUNKS[c]
        ref = gath.at[pl.ds(d * NT_DEV + off // BLK, width // BLK), which_rows, :]
        return pltpu.make_async_remote_copy(
            src_ref=ref,
            dst_ref=ref,
            send_sem=g_send.at[c, idx],
            recv_sem=g_recv.at[c, idx],
            device_id={"dp": to},
            device_id_type=MESH,
        )

    sent = []

    def go(copy):
        copy.start()
        sent.append(copy)

    def held(c, d, which_rows):
        off, width = CHUNKS[c]
        at = d * NT_DEV + off // BLK
        return jnp.concatenate([gath[at + t, which_rows] for t in range(width // BLK)], axis=1)

    def use_rows(c, d):
        off, width = CHUNKS[c]
        at = pl.ds(pl.multiple_of(d * FEAT + off, BLK), width)
        gu_acc[...] += mm(held(c, d, rows_s), wgu[at, :])

    def use_grads(c, d):
        off, width = CHUNKS[c]
        at = pl.ds(pl.multiple_of(d * FEAT + off, BLK), width)
        hg_acc[...] += mm_nt(held(c, d, grads_s), wd[:, at])

    def take_own(c):
        off, width = CHUNKS[c]
        cols = pl.ds(off, width)
        a_own[c].wait()
        rest = recv.at[pl.ds(0, nexp - 1), :, cols]
        pltpu.make_async_copy(rest, rest, a_recv.at[c]).wait()
        got = recv[:, :, cols].reshape(nexp * 16, width)
        packed = mm(compact, got).astype(BF16)
        for t in range(width // BLK):
            gath[me_d * NT_DEV + off // BLK + t] = packed[:, t * BLK : (t + 1) * BLK]
        go(part(c, 0, me_d, rows_s, right))
        go(part(c, 1, me_d, grads_s, left))
        go(part(c, 2, me_d, grads_s, right))
        go(part(c, 3, me_d, rows_s, left))
        go(part(c, 6, me_d, both, partner))
        use_rows(c, me_d)
        use_grads(c, me_d)

    def take_near_first(c):
        part(c, 0, left, rows_s, me_d).wait_recv()
        go(part(c, 4, left, rows_s, right))
        go(part(c, 7, left, rows_s, partner))
        part(c, 1, right, grads_s, me_d).wait_recv()
        go(part(c, 5, right, grads_s, left))
        go(part(c, 8, right, grads_s, partner))
        use_rows(c, left)
        use_grads(c, right)
        part(c, 6, partner, both, me_d).wait_recv()
        use_rows(c, partner)
        use_grads(c, partner)

    def take_near_second(c):
        part(c, 2, left, grads_s, me_d).wait_recv()
        go(part(c, 9, left, grads_s, partner))
        part(c, 3, right, rows_s, me_d).wait_recv()
        go(part(c, 10, right, rows_s, partner))
        use_grads(c, left)
        use_rows(c, right)
        part(c, 7, other(left), rows_s, me_d).wait_recv()
        part(c, 8, other(right), grads_s, me_d).wait_recv()
        use_rows(c, other(left))
        use_grads(c, other(right))

    def take_far(c):
        part(c, 4, far, rows_s, me_d).wait_recv()
        go(part(c, 11, far, rows_s, partner))
        part(c, 5, far, grads_s, me_d).wait_recv()
        go(part(c, 12, far, grads_s, partner))
        use_rows(c, far)
        use_grads(c, far)
        part(c, 9, other(left), grads_s, me_d).wait_recv()
        part(c, 10, other(right), rows_s, me_d).wait_recv()
        use_grads(c, other(left))
        use_rows(c, other(right))

    def take_last(c):
        part(c, 11, other(far), rows_s, me_d).wait_recv()
        use_rows(c, other(far))
        part(c, 12, other(far), grads_s, me_d).wait_recv()
        use_grads(c, other(far))

    take_own(0)
    take_near_first(0)
    take_own(1)
    take_near_second(0)
    take_far(0)
    take_near_first(1)
    take_last(0)
    take_near_second(1)
    take_far(1)
    take_last(1)

    gate_pre = gu_acc[:, :HID]
    up_pre = gu_acc[:, HID:]
    hidden_grad = hg_acc[...]
    sig = jax.nn.sigmoid(gate_pre)
    swish = gate_pre * sig
    hid_b[...] = (swish * up_pre).astype(BF16)
    gu_b[:, :HID] = (hidden_grad * up_pre * sig * (1.0 + gate_pre * (1.0 - sig))).astype(BF16)
    gu_b[:, HID:] = (hidden_grad * swish).astype(BF16)

    targets = (far, right, left, me_d)

    def term(c, d):
        off, width = CHUNKS[c]
        at = pl.ds(pl.multiple_of(d * FEAT + off, BLK), width)
        return mm_nt(gu_b[...], wgu[at, :])

    def pair(c, j):
        cols = pl.ds(*CHUNKS[c])
        return pltpu.make_async_remote_copy(
            src_ref=p_send.at[j, :, cols],
            dst_ref=p_recv.at[j, :, cols],
            send_sem=p_ssem.at[c, j],
            recv_sem=p_rsem.at[c, j],
            device_id={"dp": partner},
            device_id_type=MESH,
        )

    def ring(c, idx, src, dst, to):
        return pltpu.make_async_remote_copy(
            src_ref=src,
            dst_ref=dst,
            send_sem=x_ssem.at[c, idx],
            recv_sem=x_rsem.at[c, idx],
            device_id={"dp": to},
            device_id_type=MESH,
        )

    low = pl.ds(0, HALF)
    high = pl.ds(HALF, HALF)

    def ring_copies(c):
        cols = pl.ds(*CHUNKS[c])
        return (
            ring(c, 0, far_s.at[low, cols], far_l.at[:, cols], right),
            ring(c, 1, far_s.at[high, cols], far_r.at[:, cols], left),
            ring(c, 2, right_s.at[high, cols], from_l.at[high, cols], right),
            ring(c, 3, left_s.at[low, cols], from_r.at[low, cols], left),
            ring(c, 4, right_s.at[low, cols], from_l.at[low, cols], right),
            ring(c, 5, left_s.at[high, cols], from_r.at[high, cols], left),
        )

    def give_partner(c, j):
        cols = pl.ds(*CHUNKS[c])
        p_send[j, :, cols] = term(c, other(targets[j])).astype(BF16)
        go(pair(c, j))

    def summed(c, j):
        cols = pl.ds(*CHUNKS[c])
        value = term(c, targets[j])
        pair(c, j).wait_recv()
        return value + p_recv[j, :, cols].astype(F32)

    def ring_first(c):
        cols = pl.ds(*CHUNKS[c])
        copies = ring_copies(c)
        far_s[:, cols] = summed(c, 0).astype(BF16)
        go(copies[0])
        go(copies[1])
        value = summed(c, 1)
        right_s[high, cols] = value[HALF:].astype(BF16)
        go(copies[2])
        right_t[:, cols] = value[:HALF]
        value = summed(c, 2)
        left_s[low, cols] = value[:HALF].astype(BF16)
        go(copies[3])
        left_t[:, cols] = value[HALF:]

    def ring_second(c):
        cols = pl.ds(*CHUNKS[c])
        copies = ring_copies(c)
        copies[0].wait_recv()
        right_s[low, cols] = (right_t[:, cols] + far_l[:, cols].astype(F32)).astype(BF16)
        go(copies[4])
        copies[1].wait_recv()
        left_s[high, cols] = (left_t[:, cols] + far_r[:, cols].astype(F32)).astype(BF16)
        go(copies[5])

    back_row = lax.broadcasted_iota(jnp.int32, (nexp * PAD, ROWS), 0)
    back_col = lax.broadcasted_iota(jnp.int32, (nexp * PAD, ROWS), 1)
    back_r = back_row & (PAD - 1)
    spread = jnp.where(
        (back_col == (back_row >> 3) * CAP + back_r) & (back_r < CAP), 1.0, 0.0
    ).astype(BF16)
    d_own = []

    def give_back(c):
        off, width = CHUNKS[c]
        cols = pl.ds(off, width)
        copies = ring_copies(c)
        for i in (2, 3, 4, 5):
            copies[i].wait_recv()
        total = own_t[:, cols] + from_l[:, cols].astype(F32) + from_r[:, cols].astype(F32)
        wide = mm(spread, total.astype(BF16)).reshape(nexp, PAD, width)
        second = wide[:, :, WIDE:]
        if width < 2 * WIDE:
            second = jnp.concatenate(
                [second, jnp.zeros((nexp, PAD, 2 * WIDE - width), F32)], axis=2
            )
        msg_d[c] = jnp.concatenate([wide[:, :, :WIDE], second], axis=1).astype(BF16)

        def send(i, carry):
            to = lax.rem(me_e + i, nexp)
            pltpu.make_async_remote_copy(
                src_ref=msg_d.at[c, to],
                dst_ref=recv_d.at[c, me_e],
                send_sem=d_send.at[c],
                recv_sem=d_recv.at[c],
                device_id={"expert": to},
                device_id_type=MESH,
            ).start()
            return carry

        lax.fori_loop(1, nexp, send, 0)
        own = pltpu.make_async_copy(msg_d.at[c, me_e], recv_d.at[c, me_e], d_loc.at[c])
        own.start()
        d_own.append(own)

    for j in range(4):
        give_partner(0, j)
    ring_first(0)
    for j in range(4):
        give_partner(1, j)
    ring_first(1)
    ring_second(0)
    for c in range(NCH):
        own_t[:, pl.ds(*CHUNKS[c])] = summed(c, 3)
    ring_second(1)

    loads[6].wait()
    loads[7].wait()
    for c in range(2):
        lanes = pl.ds(c * BLK, BLK)
        h_part = hid_b[:, lanes]
        g_part = gu_b[:, lanes]
        u_part = gu_b[:, pl.ds(HID + c * BLK, BLK)]
        for m in range(2):
            ident = bids[0, c, m]
            kind = jnp.where(ident >= 2 * FBLK, 2, jnp.where(ident >= FBLK, 1, 0))
            rows_both = gath[ident - kind * FBLK]
            x_part = rows_both[:ROWS]
            y_part = rows_both[ROWS:]
            lhs = jnp.where(kind == 2, h_part, x_part)
            rhs = jnp.where(kind == 0, g_part, jnp.where(kind == 1, u_part, y_part))
            scale = jnp.where(kind == 2, FF**-0.5, D**-0.5).astype(F32)
            grad = mm_tn(lhs, rhs) * scale
            mom_one = beta_one * m1_v[c, m] + (1.0 - beta_one) * grad
            mom_two = beta_two * m2_v[c, m] + (1.0 - beta_two) * grad * grad
            new_delta[0, c, m] = delta_v[c, m] - learn_rate * (mom_one / corr_one) / (
                jnp.sqrt(mom_two / corr_two) + adam_eps
            )

    chosen_d, _ = slot_matrix(ids_t, gates_t, nexp * 16, 4)
    place = lax.broadcasted_iota(jnp.int32, (nexp * 16, TOK), 0) & PAD
    upper = jnp.where(place == 0, chosen_d, 0.0).T.astype(BF16)
    lower = jnp.where(place == 0, 0.0, chosen_d).T.astype(BF16)

    for c in range(NCH):
        give_back(c)
    for c, (off, width) in enumerate(CHUNKS):
        d_own[c].wait()
        rest = recv_d.at[c, pl.ds(0, nexp - 1)]
        pltpu.make_async_copy(rest, rest, d_recv.at[c]).wait()
        got = recv_d[c].reshape(nexp * 16, WIDE)
        in_grad[:, pl.ds(off, WIDE)] = mm(upper, got).astype(BF16)
        tail = width - WIDE
        in_grad[:, pl.ds(off + WIDE, tail)] = mm(lower, got[:, :tail]).astype(BF16)

    for copy in sent:
        copy.wait_send()
    for c, (off, width) in enumerate(CHUNKS):
        rest = msg.at[pl.ds(0, nexp - 1), :, pl.ds(off, width)]
        pltpu.make_async_copy(rest, rest, a_send.at[c]).wait()
        rest = msg_d.at[c, pl.ds(0, nexp - 1)]
        pltpu.make_async_copy(rest, rest, d_send.at[c]).wait()


def on_device(
    nexp,
    ndp,
    tokens,
    out_grad,
    expert_ids,
    gate_weights,
    base_gate,
    base_up,
    base_down,
    block_ids,
    delta,
    moment_one,
    moment_two,
):
    vmem = pl.BlockSpec(memory_space=pltpu.VMEM)
    smem = pl.BlockSpec(memory_space=pltpu.SMEM)
    anym = pl.BlockSpec(memory_space=pl.ANY)
    dma = pltpu.SemaphoreType.DMA
    scratch = [
        pltpu.VMEM((TOK, FEAT), BF16),
        pltpu.VMEM((TOK, FEAT), BF16),
        pltpu.VMEM((nexp, 16, FEAT), BF16),
        pltpu.VMEM((nexp, 16, FEAT), BF16),
        pltpu.VMEM((FBLK, 2 * ROWS, BLK), BF16),
        pltpu.VMEM((D, 2 * HID), BF16),
        pltpu.VMEM((HID, D), BF16),
        pltpu.VMEM((2, 2, BLK, BLK), F32),
        pltpu.VMEM((2, 2, BLK, BLK), F32),
        pltpu.VMEM((2, 2, BLK, BLK), F32),
        pltpu.VMEM((6, BLK, BLK), F32),
        pltpu.VMEM((ROWS, 2 * HID), F32),
        pltpu.VMEM((ROWS, HID), F32),
        pltpu.VMEM((ROWS, 2 * HID), BF16),
        pltpu.VMEM((ROWS, HID), BF16),
        pltpu.VMEM((4, ROWS, FEAT), BF16),
        pltpu.VMEM((4, ROWS, FEAT), BF16),
        pltpu.VMEM((ROWS, FEAT), BF16),
        pltpu.VMEM((ROWS, FEAT), BF16),
        pltpu.VMEM((ROWS, FEAT), BF16),
        pltpu.VMEM((HALF, FEAT), F32),
        pltpu.VMEM((HALF, FEAT), F32),
        pltpu.VMEM((ROWS, FEAT), F32),
        pltpu.VMEM((HALF, FEAT), BF16),
        pltpu.VMEM((HALF, FEAT), BF16),
        pltpu.VMEM((ROWS, FEAT), BF16),
        pltpu.VMEM((ROWS, FEAT), BF16),
        pltpu.VMEM((NCH, nexp, 16, WIDE), BF16),
        pltpu.VMEM((NCH, nexp, 16, WIDE), BF16),
        dma((8,)),
        dma((NCH,)),
        dma((NCH,)),
        dma((NCH,)),
        dma((NCH, 13)),
        dma((NCH, 13)),
        dma((NCH, 4)),
        dma((NCH, 4)),
        dma((NCH, 6)),
        dma((NCH, 6)),
        dma((NCH,)),
        dma((NCH,)),
        dma((NCH,)),
    ]
    return pl.pallas_call(
        functools.partial(kernel, nexp, ndp),
        out_shape=(
            jax.ShapeDtypeStruct((TOK, FEAT), BF16),
            jax.ShapeDtypeStruct((1, 2, 2, BLK, BLK), F32),
        ),
        in_specs=[vmem, vmem, smem] + [anym] * 8,
        out_specs=(vmem, vmem),
        scratch_shapes=scratch,
        compiler_params=pltpu.CompilerParams(
            collective_id=0, has_side_effects=True, vmem_limit_bytes=56 * 1024 * 1024
        ),
    )(
        expert_ids.T,
        gate_weights.T,
        block_ids,
        tokens,
        out_grad,
        base_gate,
        base_up,
        base_down,
        delta,
        moment_one,
        moment_two,
    )


def solution(mesh):
    placed = (
        P("expert", None),
        P("expert", None),
        P("expert", None),
        P("expert", None),
        P("expert", None, "dp"),
        P("expert", None, "dp"),
        P("expert", "dp", None),
        P("expert", "dp", None),
        P("expert", "dp", None, None, None),
        P("expert", "dp", None, None, None),
        P("expert", "dp", None, None, None),
    )
    return jax.shard_map(
        functools.partial(on_device, mesh.shape["expert"], mesh.shape["dp"]),
        mesh=mesh,
        in_specs=placed,
        out_specs=(P("expert", "dp"), P("expert", "dp", None, None, None)),
        check_vma=False,
    )
```

```python
import functools

import jax
import jax.numpy as jnp
from jax import lax
from jax.experimental import pallas as pl
from jax.experimental.pallas import tpu as pltpu
from jax.sharding import PartitionSpec as P

D = 7168
FF = 2048
BLK = 128
CAP = 6
PAD = 8
TOK = 16
TOP = 8
HID = 256
ROWS = 192
HALF = ROWS // 2
FEAT = 896
FBLK = D // BLK
NT_DEV = FEAT // BLK


def cut(*widths):
    return tuple((sum(widths[:i]), w) for i, w in enumerate(widths))


CHUNKS = cut(128, 256, 256, 256)
NCH = len(CHUNKS)
GROUPS = cut(128, 256, 256, 256)
SUMS = cut(256, 256, 256, 128)
NSM = len(SUMS)
BACK = cut(256, 256, 256, 128)
NBK = len(BACK)
WIDE = 128
TAKE_KEYS = (0, 0.6, 0.65, 1.1, 1.15, 1.6, 1.65, 2.1)
GIVE_KEYS = (0, 0.5, 1.6, 2.7)

beta_one = 0.9
beta_two = 0.95
learn_rate = 0.5
adam_eps = 1e-08
corr_one = 1.0 - beta_one**10
corr_two = 1.0 - beta_two**10

MESH = pl.DeviceIdType.MESH
F32 = jnp.float32
BF16 = jnp.bfloat16
NT = (((1,), (1,)), ((), ()))
TN = (((0,), (0,)), ((), ()))


def last_of(parts, whole):
    ends = {off + width: (off, width) for off, width in whole}
    return {c: ends[off + width] for c, (off, width) in enumerate(parts) if off + width in ends}


def in_order(parts, keys):
    steps = [(c + key, c, step) for c in range(parts) for step, key in enumerate(keys)]
    return [step[1:] for step in sorted(steps)]


def mm(a, b):
    return jnp.dot(a, b, preferred_element_type=F32)


def mm_nt(a, b):
    return lax.dot_general(a, b, NT, preferred_element_type=F32)


def mm_tn(a, b):
    return lax.dot_general(a, b, TN, preferred_element_type=F32)


def slot_matrix(ids_t, gates_t, count, width_bits):
    place = lax.broadcasted_iota(jnp.int32, (count, TOK), 0)
    expert = place >> width_bits
    rank = (place & (PAD - 1)).astype(F32)
    named = jnp.zeros((count, TOK), F32)
    gates = jnp.zeros((count, TOK), F32)
    for k in range(TOP):
        hit = expert == ids_t[k : k + 1, :]
        named = jnp.where(hit, 1.0, named)
        gates = jnp.where(hit, gates_t[k : k + 1, :], gates)
    earlier = (
        lax.broadcasted_iota(jnp.int32, (TOK, TOK), 0)
        < lax.broadcasted_iota(jnp.int32, (TOK, TOK), 1)
    ).astype(F32)
    before = mm(named.astype(BF16), earlier.astype(BF16))
    chosen = jnp.where(before == rank, named, 0.0)
    return chosen, gates


def kernel(
    nexp,
    ndp,
    ids_ref,
    gates_ref,
    bids,
    tok_hbm,
    og_hbm,
    wg_hbm,
    wu_hbm,
    wd_hbm,
    delta_hbm,
    m1_hbm,
    m2_hbm,
    in_grad,
    new_delta,
    tok_v,
    og_v,
    msg,
    recv,
    gath,
    wgu,
    wd,
    delta_v,
    m1_v,
    m2_v,
    dz,
    gu_acc,
    hg_acc,
    gu_b,
    hid_b,
    p_send,
    p_recv,
    far_s,
    right_s,
    left_s,
    right_t,
    left_t,
    own_t,
    far_l,
    far_r,
    from_l,
    from_r,
    msg_d,
    recv_d,
    load_sem,
    a_send,
    a_recv,
    a_loc,
    g_send,
    g_recv,
    p_ssem,
    p_rsem,
    x_ssem,
    x_rsem,
    d_send,
    d_recv,
    d_loc,
):
    me_d = lax.axis_index("dp")
    me_e = lax.axis_index("expert")
    core = lax.rem(me_d, 2)
    flip = 1 - 2 * core
    partner = me_d + flip
    right = lax.rem(me_d + 2, ndp)
    left = lax.rem(me_d + ndp - 2, ndp)
    far = lax.rem(me_d + 4, ndp)

    barrier = pltpu.get_barrier_semaphore()

    def greet(i, carry):
        pl.semaphore_signal(
            barrier, inc=1, device_id={"expert": lax.rem(me_e + i, nexp)}, device_id_type=MESH
        )
        return carry

    lax.fori_loop(1, nexp, greet, 0)
    for other in (partner, right, left):
        pl.semaphore_signal(barrier, inc=1, device_id={"dp": other}, device_id_type=MESH)

    first = pl.multiple_of(me_d * FEAT, BLK)
    loads = [
        pltpu.make_async_copy(tok_hbm.at[:, pl.ds(first, FEAT)], tok_v, load_sem.at[0]),
        pltpu.make_async_copy(og_hbm.at[:, pl.ds(first, FEAT)], og_v, load_sem.at[1]),
        pltpu.make_async_copy(delta_hbm.at[0], delta_v, load_sem.at[2]),
        pltpu.make_async_copy(wg_hbm.at[0], wgu.at[:, pl.ds(0, HID)], load_sem.at[3]),
        pltpu.make_async_copy(wu_hbm.at[0], wgu.at[:, pl.ds(HID, HID)], load_sem.at[4]),
        pltpu.make_async_copy(wd_hbm.at[0], wd, load_sem.at[5]),
        pltpu.make_async_copy(m1_hbm.at[0], m1_v, load_sem.at[6]),
        pltpu.make_async_copy(m2_hbm.at[0], m2_v, load_sem.at[7]),
    ]
    for load in loads:
        load.start()

    ids_t = ids_ref[...]
    gates_t = gates_ref[...]
    chosen, gates = slot_matrix(ids_t, gates_t, nexp * PAD, 3)
    gate_of = jnp.sum(chosen * gates, axis=1, keepdims=True)
    chosen_b = chosen.astype(BF16)
    loads[0].wait()
    loads[1].wait()
    for off, width in CHUNKS:
        cols = pl.ds(off, width)
        rows_out = mm(chosen_b, tok_v[:, cols])
        grads_out = mm(chosen_b, og_v[:, cols]) * gate_of
        msg[:, :, cols] = jnp.concatenate(
            [rows_out.reshape(nexp, PAD, width), grads_out.reshape(nexp, PAD, width)], axis=1
        ).astype(BF16)

    pl.semaphore_wait(barrier, nexp - 1 + 3)

    a_own = []
    for c, (off, width) in enumerate(CHUNKS):
        cols = pl.ds(off, width)

        def send(i, carry, c=c, cols=cols):
            to = lax.rem(me_e + i, nexp)
            pltpu.make_async_remote_copy(
                src_ref=msg.at[to, :, cols],
                dst_ref=recv.at[me_e, :, cols],
                send_sem=a_send.at[c],
                recv_sem=a_recv.at[c],
                device_id={"expert": to},
                device_id_type=MESH,
            ).start()
            return carry

        lax.fori_loop(1, nexp, send, 0)
        own = pltpu.make_async_copy(msg.at[me_e, :, cols], recv.at[me_e, :, cols], a_loc.at[c])
        own.start()
        a_own.append(own)

    def adjust_all():
        loads[2].wait()
        for c in range(2):
            for m in range(2):
                scale = jnp.where(bids[0, c, m] >= 2 * FBLK, FF**-0.5, D**-0.5).astype(F32)
                dz[3 * c + m] = delta_v[c, m] * scale
            dz[3 * c + 2] = jnp.zeros((BLK, BLK), F32)
        for i in (3, 4, 5):
            loads[i].wait()

        def which(c, want):
            return 3 * c + jnp.where(bids[0, c, 0] == want, 0, jnp.where(bids[0, c, 1] == want, 1, 2))

        def adjust(j, carry):
            at = pl.ds(pl.multiple_of(j * BLK, BLK), BLK)
            for kind in range(2):
                for c in range(2):
                    lanes = pl.ds(kind * HID + c * BLK, BLK)
                    old = wgu[at, lanes].astype(F32)
                    wgu[at, lanes] = (old + dz[which(c, kind * FBLK + j)]).astype(BF16)
            for c in range(2):
                subl = pl.ds(c * BLK, BLK)
                old = wd[subl, at].astype(F32)
                wd[subl, at] = (old + dz[which(c, 2 * FBLK + j)]).astype(BF16)
            return carry

        lax.fori_loop(0, FBLK, adjust, 0)

    adjust_all()

    chosen_d, _ = slot_matrix(ids_t, gates_t, nexp * 16, 4)
    place = lax.broadcasted_iota(jnp.int32, (nexp * 16, TOK), 0) & PAD
    upper = jnp.where(place == 0, chosen_d, 0.0).T.astype(BF16)
    lower = jnp.where(place == 0, 0.0, chosen_d).T.astype(BF16)

    gu_acc[...] = jnp.zeros_like(gu_acc)
    hg_acc[...] = jnp.zeros_like(hg_acc)

    row_i = lax.broadcasted_iota(jnp.int32, (2 * ROWS, nexp * 16), 0)
    col_i = lax.broadcasted_iota(jnp.int32, (2 * ROWS, nexp * 16), 1)
    col_r = col_i & (PAD - 1)
    want = (col_i >> 4) * CAP + col_r + jnp.where((col_i & PAD) != 0, ROWS, 0)
    compact = jnp.where((row_i == want) & (col_r < CAP), 1.0, 0.0).astype(BF16)

    def other(d):
        return d + flip

    both = pl.ds(0, 2 * ROWS)
    rows_s = pl.ds(0, ROWS)
    grads_s = pl.ds(ROWS, ROWS)

    def part(c, idx, d, which_rows, to):
        off, width = CHUNKS[c]
        ref = gath.at[pl.ds(d * NT_DEV + off // BLK, width // BLK), which_rows, :]
        return pltpu.make_async_remote_copy(
            src_ref=ref,
            dst_ref=ref,
            send_sem=g_send.at[c, idx],
            recv_sem=g_recv.at[c, idx],
            device_id={"dp": to},
            device_id_type=MESH,
        )

    sent = []

    def go(copy):
        copy.start()
        sent.append(copy)

    def held(off, width, d, which_rows):
        at = d * NT_DEV + off // BLK
        return jnp.concatenate([gath[at + t, which_rows] for t in range(width // BLK)], axis=1)

    group_of = last_of(CHUNKS, GROUPS)

    def use_rows(c, d):
        if c in group_of:
            off, width = group_of[c]
            at = pl.ds(pl.multiple_of(d * FEAT + off, BLK), width)
            gu_acc[...] += mm(held(off, width, d, rows_s), wgu[at, :])

    def use_grads(c, d):
        if c in group_of:
            off, width = group_of[c]
            at = pl.ds(pl.multiple_of(d * FEAT + off, BLK), width)
            hg_acc[...] += mm_nt(held(off, width, d, grads_s), wd[:, at])

    def take_own(c):
        off, width = CHUNKS[c]
        cols = pl.ds(off, width)
        a_own[c].wait()
        rest = recv.at[pl.ds(0, nexp - 1), :, cols]
        pltpu.make_async_copy(rest, rest, a_recv.at[c]).wait()
        got = recv[:, :, cols].reshape(nexp * 16, width)
        packed = mm(compact, got).astype(BF16)
        for t in range(width // BLK):
            gath[me_d * NT_DEV + off // BLK + t] = packed[:, t * BLK : (t + 1) * BLK]
        go(part(c, 0, me_d, rows_s, right))
        go(part(c, 1, me_d, grads_s, left))
        go(part(c, 2, me_d, grads_s, right))
        go(part(c, 3, me_d, rows_s, left))
        go(part(c, 6, me_d, both, partner))
        use_rows(c, me_d)
        use_grads(c, me_d)

    def take_near_first(c):
        part(c, 0, left, rows_s, me_d).wait_recv()
        go(part(c, 4, left, rows_s, right))
        go(part(c, 7, left, rows_s, partner))
        part(c, 1, right, grads_s, me_d).wait_recv()
        go(part(c, 5, right, grads_s, left))
        go(part(c, 8, right, grads_s, partner))
        use_rows(c, left)
        use_grads(c, right)

    def take_partner(c):
        part(c, 6, partner, both, me_d).wait_recv()
        use_rows(c, partner)
        use_grads(c, partner)

    def take_near_second(c):
        part(c, 2, left, grads_s, me_d).wait_recv()
        go(part(c, 9, left, grads_s, partner))
        part(c, 3, right, rows_s, me_d).wait_recv()
        go(part(c, 10, right, rows_s, partner))
        use_grads(c, left)
        use_rows(c, right)

    def take_passed_first(c):
        part(c, 7, other(left), rows_s, me_d).wait_recv()
        part(c, 8, other(right), grads_s, me_d).wait_recv()
        use_rows(c, other(left))
        use_grads(c, other(right))

    def take_far(c):
        part(c, 4, far, rows_s, me_d).wait_recv()
        go(part(c, 11, far, rows_s, partner))
        part(c, 5, far, grads_s, me_d).wait_recv()
        go(part(c, 12, far, grads_s, partner))
        use_rows(c, far)
        use_grads(c, far)

    def take_passed_second(c):
        part(c, 9, other(left), grads_s, me_d).wait_recv()
        part(c, 10, other(right), rows_s, me_d).wait_recv()
        use_grads(c, other(left))
        use_rows(c, other(right))

    def take_passed_far(c):
        part(c, 11, other(far), rows_s, me_d).wait_recv()
        use_rows(c, other(far))
        part(c, 12, other(far), grads_s, me_d).wait_recv()
        use_grads(c, other(far))

    takes = (
        take_own,
        take_near_first,
        take_partner,
        take_near_second,
        take_passed_first,
        take_far,
        take_passed_second,
        take_passed_far,
    )
    for c, step in in_order(NCH, TAKE_KEYS):
        takes[step](c)

    gate_pre = gu_acc[:, :HID]
    up_pre = gu_acc[:, HID:]
    hidden_grad = hg_acc[...]
    sig = jax.nn.sigmoid(gate_pre)
    swish = gate_pre * sig
    hid_b[...] = (swish * up_pre).astype(BF16)
    gu_b[:, :HID] = (hidden_grad * up_pre * sig * (1.0 + gate_pre * (1.0 - sig))).astype(BF16)
    gu_b[:, HID:] = (hidden_grad * swish).astype(BF16)

    targets = (far, right, left, me_d)

    def term(c, d):
        off, width = SUMS[c]
        at = pl.ds(pl.multiple_of(d * FEAT + off, BLK), width)
        return mm_nt(gu_b[...], wgu[at, :])

    def pair(c, j):
        cols = pl.ds(*SUMS[c])
        return pltpu.make_async_remote_copy(
            src_ref=p_send.at[j, :, cols],
            dst_ref=p_recv.at[j, :, cols],
            send_sem=p_ssem.at[c, j],
            recv_sem=p_rsem.at[c, j],
            device_id={"dp": partner},
            device_id_type=MESH,
        )

    def ring(c, idx, src, dst, to):
        return pltpu.make_async_remote_copy(
            src_ref=src,
            dst_ref=dst,
            send_sem=x_ssem.at[c, idx],
            recv_sem=x_rsem.at[c, idx],
            device_id={"dp": to},
            device_id_type=MESH,
        )

    low = pl.ds(0, HALF)
    high = pl.ds(HALF, HALF)

    def ring_copies(c):
        cols = pl.ds(*SUMS[c])
        return (
            ring(c, 0, far_s.at[low, cols], far_l.at[:, cols], right),
            ring(c, 1, far_s.at[high, cols], far_r.at[:, cols], left),
            ring(c, 2, right_s.at[high, cols], from_l.at[high, cols], right),
            ring(c, 3, left_s.at[low, cols], from_r.at[low, cols], left),
            ring(c, 4, right_s.at[low, cols], from_l.at[low, cols], right),
            ring(c, 5, left_s.at[high, cols], from_r.at[high, cols], left),
        )

    def give_partner(c, j):
        cols = pl.ds(*SUMS[c])
        p_send[j, :, cols] = term(c, other(targets[j])).astype(BF16)
        go(pair(c, j))

    def summed(c, j):
        cols = pl.ds(*SUMS[c])
        value = term(c, targets[j])
        pair(c, j).wait_recv()
        return value + p_recv[j, :, cols].astype(F32)

    def ring_first(c):
        cols = pl.ds(*SUMS[c])
        copies = ring_copies(c)
        far_s[:, cols] = summed(c, 0).astype(BF16)
        go(copies[0])
        go(copies[1])
        value = summed(c, 1)
        right_s[high, cols] = value[HALF:].astype(BF16)
        go(copies[2])
        right_t[:, cols] = value[:HALF]
        value = summed(c, 2)
        left_s[low, cols] = value[:HALF].astype(BF16)
        go(copies[3])
        left_t[:, cols] = value[HALF:]

    def ring_second(c):
        cols = pl.ds(*SUMS[c])
        copies = ring_copies(c)
        copies[0].wait_recv()
        right_s[low, cols] = (right_t[:, cols] + far_l[:, cols].astype(F32)).astype(BF16)
        go(copies[4])
        copies[1].wait_recv()
        left_s[high, cols] = (left_t[:, cols] + far_r[:, cols].astype(F32)).astype(BF16)
        go(copies[5])
        own_t[:, cols] = summed(c, 3)

    back_row = lax.broadcasted_iota(jnp.int32, (nexp * PAD, ROWS), 0)
    back_col = lax.broadcasted_iota(jnp.int32, (nexp * PAD, ROWS), 1)
    back_r = back_row & (PAD - 1)
    spread = jnp.where(
        (back_col == (back_row >> 3) * CAP + back_r) & (back_r < CAP), 1.0, 0.0
    ).astype(BF16)
    d_own = []

    def give_back(c):
        off, width = BACK[c]
        cols = pl.ds(off, width)
        for p, (low_end, size) in enumerate(SUMS):
            if off <= low_end < off + width:
                for copy in ring_copies(p)[2:]:
                    copy.wait_recv()
        total = own_t[:, cols] + from_l[:, cols].astype(F32) + from_r[:, cols].astype(F32)
        wide = mm(spread, total.astype(BF16)).reshape(nexp, PAD, width)
        second = wide[:, :, WIDE:] if width > WIDE else jnp.zeros((nexp, PAD, WIDE), F32)
        msg_d[c] = jnp.concatenate([wide[:, :, :WIDE], second], axis=1).astype(BF16)

        def send(i, carry):
            to = lax.rem(me_e + i, nexp)
            pltpu.make_async_remote_copy(
                src_ref=msg_d.at[c, to],
                dst_ref=recv_d.at[c, me_e],
                send_sem=d_send.at[c],
                recv_sem=d_recv.at[c],
                device_id={"expert": to},
                device_id_type=MESH,
            ).start()
            return carry

        lax.fori_loop(1, nexp, send, 0)
        own = pltpu.make_async_copy(msg_d.at[c, me_e], recv_d.at[c, me_e], d_loc.at[c])
        own.start()
        d_own.append(own)

    def give_partner_all(c):
        for j in range(4):
            give_partner(c, j)

    ends = last_of(SUMS, BACK)

    def finish(c):
        if c in ends:
            give_back(BACK.index(ends[c]))

    gives = (give_partner_all, ring_first, ring_second, finish)
    for c, step in in_order(NSM, GIVE_KEYS):
        gives[step](c)

    loads[6].wait()
    loads[7].wait()
    for c in range(2):
        lanes = pl.ds(c * BLK, BLK)
        h_part = hid_b[:, lanes]
        g_part = gu_b[:, lanes]
        u_part = gu_b[:, pl.ds(HID + c * BLK, BLK)]
        for m in range(2):
            ident = bids[0, c, m]
            kind = jnp.where(ident >= 2 * FBLK, 2, jnp.where(ident >= FBLK, 1, 0))
            rows_both = gath[ident - kind * FBLK]
            x_part = rows_both[:ROWS]
            y_part = rows_both[ROWS:]
            lhs = jnp.where(kind == 2, h_part, x_part)
            rhs = jnp.where(kind == 0, g_part, jnp.where(kind == 1, u_part, y_part))
            scale = jnp.where(kind == 2, FF**-0.5, D**-0.5).astype(F32)
            grad = mm_tn(lhs, rhs) * scale
            mom_one = beta_one * m1_v[c, m] + (1.0 - beta_one) * grad
            mom_two = beta_two * m2_v[c, m] + (1.0 - beta_two) * grad * grad
            new_delta[0, c, m] = delta_v[c, m] - learn_rate * (mom_one / corr_one) / (
                jnp.sqrt(mom_two / corr_two) + adam_eps
            )

    for c, (off, width) in enumerate(BACK):
        d_own[c].wait()
        rest = recv_d.at[c, pl.ds(0, nexp - 1)]
        pltpu.make_async_copy(rest, rest, d_recv.at[c]).wait()
        got = recv_d[c].reshape(nexp * 16, WIDE)
        in_grad[:, pl.ds(off, WIDE)] = mm(upper, got).astype(BF16)
        if width > WIDE:
            in_grad[:, pl.ds(off + WIDE, WIDE)] = mm(lower, got).astype(BF16)

    for copy in sent:
        copy.wait_send()
    for c, (off, width) in enumerate(CHUNKS):
        rest = msg.at[pl.ds(0, nexp - 1), :, pl.ds(off, width)]
        pltpu.make_async_copy(rest, rest, a_send.at[c]).wait()
    for c in range(NBK):
        rest = msg_d.at[c, pl.ds(0, nexp - 1)]
        pltpu.make_async_copy(rest, rest, d_send.at[c]).wait()


def hand_on(grad_in, delta_in, grad_out, delta_out):
    grad_out[...] = grad_in[...]
    delta_out[...] = delta_in[...]


def on_device(
    nexp,
    ndp,
    tokens,
    out_grad,
    expert_ids,
    gate_weights,
    base_gate,
    base_up,
    base_down,
    block_ids,
    delta,
    moment_one,
    moment_two,
):
    vmem = pl.BlockSpec(memory_space=pltpu.VMEM)
    smem = pl.BlockSpec(memory_space=pltpu.SMEM)
    anym = pl.BlockSpec(memory_space=pl.ANY)
    dma = pltpu.SemaphoreType.DMA
    scratch = [
        pltpu.VMEM((TOK, FEAT), BF16),
        pltpu.VMEM((TOK, FEAT), BF16),
        pltpu.VMEM((nexp, 16, FEAT), BF16),
        pltpu.VMEM((nexp, 16, FEAT), BF16),
        pltpu.VMEM((FBLK, 2 * ROWS, BLK), BF16),
        pltpu.VMEM((D, 2 * HID), BF16),
        pltpu.VMEM((HID, D), BF16),
        pltpu.VMEM((2, 2, BLK, BLK), F32),
        pltpu.VMEM((2, 2, BLK, BLK), F32),
        pltpu.VMEM((2, 2, BLK, BLK), F32),
        pltpu.VMEM((6, BLK, BLK), F32),
        pltpu.VMEM((ROWS, 2 * HID), F32),
        pltpu.VMEM((ROWS, HID), F32),
        pltpu.VMEM((ROWS, 2 * HID), BF16),
        pltpu.VMEM((ROWS, HID), BF16),
        pltpu.VMEM((4, ROWS, FEAT), BF16),
        pltpu.VMEM((4, ROWS, FEAT), BF16),
        pltpu.VMEM((ROWS, FEAT), BF16),
        pltpu.VMEM((ROWS, FEAT), BF16),
        pltpu.VMEM((ROWS, FEAT), BF16),
        pltpu.VMEM((HALF, FEAT), F32),
        pltpu.VMEM((HALF, FEAT), F32),
        pltpu.VMEM((ROWS, FEAT), F32),
        pltpu.VMEM((HALF, FEAT), BF16),
        pltpu.VMEM((HALF, FEAT), BF16),
        pltpu.VMEM((ROWS, FEAT), BF16),
        pltpu.VMEM((ROWS, FEAT), BF16),
        pltpu.VMEM((NBK, nexp, 16, WIDE), BF16),
        pltpu.VMEM((NBK, nexp, 16, WIDE), BF16),
        dma((8,)),
        dma((NCH,)),
        dma((NCH,)),
        dma((NCH,)),
        dma((NCH, 13)),
        dma((NCH, 13)),
        dma((NSM, 4)),
        dma((NSM, 4)),
        dma((NSM, 6)),
        dma((NSM, 6)),
        dma((NBK,)),
        dma((NBK,)),
        dma((NBK,)),
    ]
    in_grad, new_delta = pl.pallas_call(
        functools.partial(kernel, nexp, ndp),
        out_shape=(
            jax.ShapeDtypeStruct((TOK, FEAT), BF16),
            jax.ShapeDtypeStruct((1, 2, 2, BLK, BLK), F32),
        ),
        in_specs=[vmem, vmem, smem] + [anym] * 8,
        out_specs=(vmem, vmem),
        scratch_shapes=scratch,
        compiler_params=pltpu.CompilerParams(
            collective_id=0, has_side_effects=True, vmem_limit_bytes=56 * 1024 * 1024
        ),
    )(
        expert_ids.T,
        gate_weights.T,
        block_ids,
        tokens,
        out_grad,
        base_gate,
        base_up,
        base_down,
        delta,
        moment_one,
        moment_two,
    )
    return pl.pallas_call(
        hand_on,
        out_shape=(
            jax.ShapeDtypeStruct(in_grad.shape, in_grad.dtype),
            jax.ShapeDtypeStruct(new_delta.shape, new_delta.dtype),
        ),
        in_specs=[vmem, vmem],
        out_specs=(vmem, vmem),
    )(in_grad, new_delta)


def solution(mesh):
    placed = (
        P("expert", None),
        P("expert", None),
        P("expert", None),
        P("expert", None),
        P("expert", None, "dp"),
        P("expert", None, "dp"),
        P("expert", "dp", None),
        P("expert", "dp", None),
        P("expert", "dp", None, None, None),
        P("expert", "dp", None, None, None),
        P("expert", "dp", None, None, None),
    )
    return jax.shard_map(
        functools.partial(on_device, mesh.shape["expert"], mesh.shape["dp"]),
        mesh=mesh,
        in_specs=placed,
        out_specs=(P("expert", "dp"), P("expert", "dp", None, None, None)),
        check_vma=False,
    )
```

```python
import functools

import jax
import jax.numpy as jnp
from jax import lax
from jax.experimental import pallas as pl
from jax.experimental.pallas import tpu as pltpu
from jax.sharding import PartitionSpec as P

D = 7168
FF = 2048
BLK = 128
CAP = 6
PAD = 8
TOK = 16
TOP = 8
HID = 256
ROWS = 192
HALF = ROWS // 2
FEAT = 896
FBLK = D // BLK
NT_DEV = FEAT // BLK


def cut(*widths):
    return tuple((sum(widths[:i]), w) for i, w in enumerate(widths))


CHUNKS = cut(256, 256, 384)
NCH = len(CHUNKS)
GROUPS = cut(256, 256, 384)
SUMS = cut(256, 256, 256, 128)
NSM = len(SUMS)
BACK = cut(256, 256, 256, 128)
NBK = len(BACK)
WIDE = 128
TAKE_KEYS = (0, 0.55, 0.7, 1.05, 1.2, 1.6, 1.75, 2.1)
GIVE_KEYS = (0, 0.5, 1.6, 2.7)

beta_one = 0.9
beta_two = 0.95
learn_rate = 0.5
adam_eps = 1e-08
corr_one = 1.0 - beta_one**10
corr_two = 1.0 - beta_two**10

MESH = pl.DeviceIdType.MESH
F32 = jnp.float32
BF16 = jnp.bfloat16
NT = (((1,), (1,)), ((), ()))
TN = (((0,), (0,)), ((), ()))


def last_of(parts, whole):
    ends = {off + width: (off, width) for off, width in whole}
    return {c: ends[off + width] for c, (off, width) in enumerate(parts) if off + width in ends}


def in_order(parts, keys):
    steps = [(c + key, c, step) for c in range(parts) for step, key in enumerate(keys)]
    return [step[1:] for step in sorted(steps)]


def mm(a, b):
    return jnp.dot(a, b, preferred_element_type=F32)


def mm_nt(a, b):
    return lax.dot_general(a, b, NT, preferred_element_type=F32)


def mm_tn(a, b):
    return lax.dot_general(a, b, TN, preferred_element_type=F32)


def slot_matrix(ids_t, gates_t, count, width_bits):
    place = lax.broadcasted_iota(jnp.int32, (count, TOK), 0)
    expert = place >> width_bits
    rank = (place & (PAD - 1)).astype(F32)
    named = jnp.zeros((count, TOK), F32)
    gates = jnp.zeros((count, TOK), F32)
    for k in range(TOP):
        hit = expert == ids_t[k : k + 1, :]
        named = jnp.where(hit, 1.0, named)
        gates = jnp.where(hit, gates_t[k : k + 1, :], gates)
    earlier = (
        lax.broadcasted_iota(jnp.int32, (TOK, TOK), 0)
        < lax.broadcasted_iota(jnp.int32, (TOK, TOK), 1)
    ).astype(F32)
    before = mm(named.astype(BF16), earlier.astype(BF16))
    chosen = jnp.where(before == rank, named, 0.0)
    return chosen, gates


def kernel(
    nexp,
    ndp,
    ids_hbm,
    gates_hbm,
    bids,
    tok_hbm,
    og_hbm,
    wg_hbm,
    wu_hbm,
    wd_hbm,
    delta_hbm,
    m1_hbm,
    m2_hbm,
    in_grad,
    new_delta,
    ids_v,
    gates_v,
    tok_v,
    og_v,
    msg,
    recv,
    gath,
    wgu,
    wd,
    delta_v,
    m1_v,
    m2_v,
    dz,
    gu_acc,
    hg_acc,
    gu_b,
    hid_b,
    p_send,
    p_recv,
    far_s,
    right_s,
    left_s,
    right_t,
    left_t,
    own_t,
    far_l,
    far_r,
    from_l,
    from_r,
    msg_d,
    recv_d,
    load_sem,
    a_send,
    a_recv,
    a_loc,
    g_send,
    g_recv,
    p_ssem,
    p_rsem,
    x_ssem,
    x_rsem,
    d_send,
    d_recv,
    d_loc,
):
    me_d = lax.axis_index("dp")
    me_e = lax.axis_index("expert")
    core = lax.rem(me_d, 2)
    flip = 1 - 2 * core
    partner = me_d + flip
    right = lax.rem(me_d + 2, ndp)
    left = lax.rem(me_d + ndp - 2, ndp)
    far = lax.rem(me_d + 4, ndp)

    barrier = pltpu.get_barrier_semaphore()

    def greet(i, carry):
        pl.semaphore_signal(
            barrier, inc=1, device_id={"expert": lax.rem(me_e + i, nexp)}, device_id_type=MESH
        )
        return carry

    lax.fori_loop(1, nexp, greet, 0)
    for other in (partner, right, left):
        pl.semaphore_signal(barrier, inc=1, device_id={"dp": other}, device_id_type=MESH)

    first = pl.multiple_of(me_d * FEAT, BLK)
    loads = [
        pltpu.make_async_copy(tok_hbm.at[:, pl.ds(first, FEAT)], tok_v, load_sem.at[0]),
        pltpu.make_async_copy(og_hbm.at[:, pl.ds(first, FEAT)], og_v, load_sem.at[1]),
        pltpu.make_async_copy(delta_hbm.at[0], delta_v, load_sem.at[2]),
        pltpu.make_async_copy(wg_hbm.at[0], wgu.at[:, pl.ds(0, HID)], load_sem.at[3]),
        pltpu.make_async_copy(wu_hbm.at[0], wgu.at[:, pl.ds(HID, HID)], load_sem.at[4]),
        pltpu.make_async_copy(wd_hbm.at[0], wd, load_sem.at[5]),
        pltpu.make_async_copy(m1_hbm.at[0], m1_v, load_sem.at[6]),
        pltpu.make_async_copy(m2_hbm.at[0], m2_v, load_sem.at[7]),
    ]
    tables = [
        pltpu.make_async_copy(ids_hbm, ids_v, load_sem.at[8]),
        pltpu.make_async_copy(gates_hbm, gates_v, load_sem.at[9]),
    ]
    for load in tables + loads:
        load.start()

    for load in tables:
        load.wait()
    ids_t = ids_v[...]
    gates_t = gates_v[...]
    chosen, gates = slot_matrix(ids_t, gates_t, nexp * PAD, 3)
    gate_of = jnp.sum(chosen * gates, axis=1, keepdims=True)
    chosen_b = chosen.astype(BF16)
    loads[0].wait()
    loads[1].wait()
    def build(c):
        off, width = CHUNKS[c]
        cols = pl.ds(off, width)
        rows_out = mm(chosen_b, tok_v[:, cols])
        grads_out = mm(chosen_b, og_v[:, cols]) * gate_of
        msg[:, :, cols] = jnp.concatenate(
            [rows_out.reshape(nexp, PAD, width), grads_out.reshape(nexp, PAD, width)], axis=1
        ).astype(BF16)

    build(0)

    pl.semaphore_wait(barrier, nexp - 1 + 3)

    a_own = []
    for c, (off, width) in enumerate(CHUNKS):
        cols = pl.ds(off, width)

        def send(i, carry, c=c, cols=cols):
            to = lax.rem(me_e + i, nexp)
            pltpu.make_async_remote_copy(
                src_ref=msg.at[to, :, cols],
                dst_ref=recv.at[me_e, :, cols],
                send_sem=a_send.at[c],
                recv_sem=a_recv.at[c],
                device_id={"expert": to},
                device_id_type=MESH,
            ).start()
            return carry

        if c > 0:
            build(c)
        lax.fori_loop(1, nexp, send, 0)
        own = pltpu.make_async_copy(msg.at[me_e, :, cols], recv.at[me_e, :, cols], a_loc.at[c])
        own.start()
        a_own.append(own)

    def adjust_all():
        loads[2].wait()
        for c in range(2):
            for m in range(2):
                scale = jnp.where(bids[0, c, m] >= 2 * FBLK, FF**-0.5, D**-0.5).astype(F32)
                dz[3 * c + m] = delta_v[c, m] * scale
            dz[3 * c + 2] = jnp.zeros((BLK, BLK), F32)
        for i in (3, 4, 5):
            loads[i].wait()

        def which(c, want):
            return 3 * c + jnp.where(bids[0, c, 0] == want, 0, jnp.where(bids[0, c, 1] == want, 1, 2))

        def adjust(j, carry):
            at = pl.ds(pl.multiple_of(j * BLK, BLK), BLK)
            for kind in range(2):
                for c in range(2):
                    lanes = pl.ds(kind * HID + c * BLK, BLK)
                    old = wgu[at, lanes].astype(F32)
                    wgu[at, lanes] = (old + dz[which(c, kind * FBLK + j)]).astype(BF16)
            for c in range(2):
                subl = pl.ds(c * BLK, BLK)
                old = wd[subl, at].astype(F32)
                wd[subl, at] = (old + dz[which(c, 2 * FBLK + j)]).astype(BF16)
            return carry

        lax.fori_loop(0, FBLK, adjust, 0)

    adjust_all()

    chosen_d, _ = slot_matrix(ids_t, gates_t, nexp * 16, 4)
    place = lax.broadcasted_iota(jnp.int32, (nexp * 16, TOK), 0) & PAD
    upper = jnp.where(place == 0, chosen_d, 0.0).T.astype(BF16)
    lower = jnp.where(place == 0, 0.0, chosen_d).T.astype(BF16)

    gu_acc[...] = jnp.zeros_like(gu_acc)
    hg_acc[...] = jnp.zeros_like(hg_acc)

    row_i = lax.broadcasted_iota(jnp.int32, (2 * ROWS, nexp * 16), 0)
    col_i = lax.broadcasted_iota(jnp.int32, (2 * ROWS, nexp * 16), 1)
    col_r = col_i & (PAD - 1)
    want = (col_i >> 4) * CAP + col_r + jnp.where((col_i & PAD) != 0, ROWS, 0)
    compact = jnp.where((row_i == want) & (col_r < CAP), 1.0, 0.0).astype(BF16)

    def other(d):
        return d + flip

    both = pl.ds(0, 2 * ROWS)
    rows_s = pl.ds(0, ROWS)
    grads_s = pl.ds(ROWS, ROWS)

    def part(c, idx, d, which_rows, to):
        off, width = CHUNKS[c]
        ref = gath.at[pl.ds(d * NT_DEV + off // BLK, width // BLK), which_rows, :]
        return pltpu.make_async_remote_copy(
            src_ref=ref,
            dst_ref=ref,
            send_sem=g_send.at[c, idx],
            recv_sem=g_recv.at[c, idx],
            device_id={"dp": to},
            device_id_type=MESH,
        )

    sent = []

    def go(copy):
        copy.start()
        sent.append(copy)

    def held(off, width, d, which_rows):
        at = d * NT_DEV + off // BLK
        return jnp.concatenate([gath[at + t, which_rows] for t in range(width // BLK)], axis=1)

    group_of = last_of(CHUNKS, GROUPS)

    def use_rows(c, d):
        if c in group_of:
            off, width = group_of[c]
            at = pl.ds(pl.multiple_of(d * FEAT + off, BLK), width)
            gu_acc[...] += mm(held(off, width, d, rows_s), wgu[at, :])

    def use_grads(c, d):
        if c in group_of:
            off, width = group_of[c]
            at = pl.ds(pl.multiple_of(d * FEAT + off, BLK), width)
            hg_acc[...] += mm_nt(held(off, width, d, grads_s), wd[:, at])

    def take_own(c):
        off, width = CHUNKS[c]
        cols = pl.ds(off, width)
        a_own[c].wait()
        rest = recv.at[pl.ds(0, nexp - 1), :, cols]
        pltpu.make_async_copy(rest, rest, a_recv.at[c]).wait()
        got = recv[:, :, cols].reshape(nexp * 16, width)
        packed = mm(compact, got).astype(BF16)
        for t in range(width // BLK):
            gath[me_d * NT_DEV + off // BLK + t] = packed[:, t * BLK : (t + 1) * BLK]
        go(part(c, 0, me_d, rows_s, right))
        go(part(c, 1, me_d, grads_s, left))
        go(part(c, 2, me_d, grads_s, right))
        go(part(c, 3, me_d, rows_s, left))
        go(part(c, 6, me_d, both, partner))
        use_rows(c, me_d)
        use_grads(c, me_d)

    def take_near_first(c):
        part(c, 0, left, rows_s, me_d).wait_recv()
        go(part(c, 4, left, rows_s, right))
        go(part(c, 7, left, rows_s, partner))
        part(c, 1, right, grads_s, me_d).wait_recv()
        go(part(c, 5, right, grads_s, left))
        go(part(c, 8, right, grads_s, partner))
        use_rows(c, left)
        use_grads(c, right)

    def take_partner(c):
        part(c, 6, partner, both, me_d).wait_recv()
        use_rows(c, partner)
        use_grads(c, partner)

    def take_near_second(c):
        part(c, 2, left, grads_s, me_d).wait_recv()
        go(part(c, 9, left, grads_s, partner))
        part(c, 3, right, rows_s, me_d).wait_recv()
        go(part(c, 10, right, rows_s, partner))
        use_grads(c, left)
        use_rows(c, right)

    def take_passed_first(c):
        part(c, 7, other(left), rows_s, me_d).wait_recv()
        part(c, 8, other(right), grads_s, me_d).wait_recv()
        use_rows(c, other(left))
        use_grads(c, other(right))

    def take_far(c):
        part(c, 4, far, rows_s, me_d).wait_recv()
        go(part(c, 11, far, rows_s, partner))
        part(c, 5, far, grads_s, me_d).wait_recv()
        go(part(c, 12, far, grads_s, partner))
        use_rows(c, far)
        use_grads(c, far)

    def take_passed_second(c):
        part(c, 9, other(left), grads_s, me_d).wait_recv()
        part(c, 10, other(right), rows_s, me_d).wait_recv()
        use_grads(c, other(left))
        use_rows(c, other(right))

    def take_passed_far(c):
        part(c, 11, other(far), rows_s, me_d).wait_recv()
        use_rows(c, other(far))
        part(c, 12, other(far), grads_s, me_d).wait_recv()
        use_grads(c, other(far))

    takes = (
        take_own,
        take_near_first,
        take_partner,
        take_near_second,
        take_passed_first,
        take_far,
        take_passed_second,
        take_passed_far,
    )
    for c, step in in_order(NCH, TAKE_KEYS):
        takes[step](c)

    gate_pre = gu_acc[:, :HID]
    up_pre = gu_acc[:, HID:]
    hidden_grad = hg_acc[...]
    sig = jax.nn.sigmoid(gate_pre)
    swish = gate_pre * sig
    hid_b[...] = (swish * up_pre).astype(BF16)
    gu_b[:, :HID] = (hidden_grad * up_pre * sig * (1.0 + gate_pre * (1.0 - sig))).astype(BF16)
    gu_b[:, HID:] = (hidden_grad * swish).astype(BF16)

    targets = (far, right, left, me_d)

    def term(c, d):
        off, width = SUMS[c]
        at = pl.ds(pl.multiple_of(d * FEAT + off, BLK), width)
        return mm_nt(gu_b[...], wgu[at, :])

    def pair(c, j):
        cols = pl.ds(*SUMS[c])
        return pltpu.make_async_remote_copy(
            src_ref=p_send.at[j, :, cols],
            dst_ref=p_recv.at[j, :, cols],
            send_sem=p_ssem.at[c, j],
            recv_sem=p_rsem.at[c, j],
            device_id={"dp": partner},
            device_id_type=MESH,
        )

    def ring(c, idx, src, dst, to):
        return pltpu.make_async_remote_copy(
            src_ref=src,
            dst_ref=dst,
            send_sem=x_ssem.at[c, idx],
            recv_sem=x_rsem.at[c, idx],
            device_id={"dp": to},
            device_id_type=MESH,
        )

    low = pl.ds(0, HALF)
    high = pl.ds(HALF, HALF)

    def ring_copies(c):
        cols = pl.ds(*SUMS[c])
        return (
            ring(c, 0, far_s.at[low, cols], far_l.at[:, cols], right),
            ring(c, 1, far_s.at[high, cols], far_r.at[:, cols], left),
            ring(c, 2, right_s.at[high, cols], from_l.at[high, cols], right),
            ring(c, 3, left_s.at[low, cols], from_r.at[low, cols], left),
            ring(c, 4, right_s.at[low, cols], from_l.at[low, cols], right),
            ring(c, 5, left_s.at[high, cols], from_r.at[high, cols], left),
        )

    def give_partner(c, j):
        cols = pl.ds(*SUMS[c])
        p_send[j, :, cols] = term(c, other(targets[j])).astype(BF16)
        go(pair(c, j))

    def summed(c, j):
        cols = pl.ds(*SUMS[c])
        value = term(c, targets[j])
        pair(c, j).wait_recv()
        return value + p_recv[j, :, cols].astype(F32)

    def ring_first(c):
        cols = pl.ds(*SUMS[c])
        copies = ring_copies(c)
        far_s[:, cols] = summed(c, 0).astype(BF16)
        go(copies[0])
        go(copies[1])
        value = summed(c, 1)
        right_s[high, cols] = value[HALF:].astype(BF16)
        go(copies[2])
        right_t[:, cols] = value[:HALF]
        value = summed(c, 2)
        left_s[low, cols] = value[:HALF].astype(BF16)
        go(copies[3])
        left_t[:, cols] = value[HALF:]

    def ring_second(c):
        cols = pl.ds(*SUMS[c])
        copies = ring_copies(c)
        copies[0].wait_recv()
        right_s[low, cols] = (right_t[:, cols] + far_l[:, cols].astype(F32)).astype(BF16)
        go(copies[4])
        copies[1].wait_recv()
        left_s[high, cols] = (left_t[:, cols] + far_r[:, cols].astype(F32)).astype(BF16)
        go(copies[5])
        own_t[:, cols] = summed(c, 3)

    back_row = lax.broadcasted_iota(jnp.int32, (nexp * PAD, ROWS), 0)
    back_col = lax.broadcasted_iota(jnp.int32, (nexp * PAD, ROWS), 1)
    back_r = back_row & (PAD - 1)
    spread = jnp.where(
        (back_col == (back_row >> 3) * CAP + back_r) & (back_r < CAP), 1.0, 0.0
    ).astype(BF16)
    d_own = []

    def give_back(c):
        off, width = BACK[c]
        cols = pl.ds(off, width)
        for p, (low_end, size) in enumerate(SUMS):
            if off <= low_end < off + width:
                for copy in ring_copies(p)[2:]:
                    copy.wait_recv()
        total = own_t[:, cols] + from_l[:, cols].astype(F32) + from_r[:, cols].astype(F32)
        wide = mm(spread, total.astype(BF16)).reshape(nexp, PAD, width)
        second = wide[:, :, WIDE:] if width > WIDE else jnp.zeros((nexp, PAD, WIDE), F32)
        msg_d[c] = jnp.concatenate([wide[:, :, :WIDE], second], axis=1).astype(BF16)

        def send(i, carry):
            to = lax.rem(me_e + i, nexp)
            pltpu.make_async_remote_copy(
                src_ref=msg_d.at[c, to],
                dst_ref=recv_d.at[c, me_e],
                send_sem=d_send.at[c],
                recv_sem=d_recv.at[c],
                device_id={"expert": to},
                device_id_type=MESH,
            ).start()
            return carry

        lax.fori_loop(1, nexp, send, 0)
        own = pltpu.make_async_copy(msg_d.at[c, me_e], recv_d.at[c, me_e], d_loc.at[c])
        own.start()
        d_own.append(own)

    def give_partner_all(c):
        for j in range(4):
            give_partner(c, j)

    ends = last_of(SUMS, BACK)

    def finish(c):
        if c in ends:
            give_back(BACK.index(ends[c]))

    gives = (give_partner_all, ring_first, ring_second, finish)
    for c, step in in_order(NSM, GIVE_KEYS):
        gives[step](c)

    loads[6].wait()
    loads[7].wait()
    for c in range(2):
        lanes = pl.ds(c * BLK, BLK)
        h_part = hid_b[:, lanes]
        g_part = gu_b[:, lanes]
        u_part = gu_b[:, pl.ds(HID + c * BLK, BLK)]
        for m in range(2):
            ident = bids[0, c, m]
            kind = jnp.where(ident >= 2 * FBLK, 2, jnp.where(ident >= FBLK, 1, 0))
            rows_both = gath[ident - kind * FBLK]
            x_part = rows_both[:ROWS]
            y_part = rows_both[ROWS:]
            lhs = jnp.where(kind == 2, h_part, x_part)
            rhs = jnp.where(kind == 0, g_part, jnp.where(kind == 1, u_part, y_part))
            scale = jnp.where(kind == 2, FF**-0.5, D**-0.5).astype(F32)
            grad = mm_tn(lhs, rhs) * scale
            mom_one = beta_one * m1_v[c, m] + (1.0 - beta_one) * grad
            mom_two = beta_two * m2_v[c, m] + (1.0 - beta_two) * grad * grad
            new_delta[0, c, m] = delta_v[c, m] - learn_rate * (mom_one / corr_one) / (
                jnp.sqrt(mom_two / corr_two) + adam_eps
            )

    for copy in sent:
        copy.wait_send()
    for c, (off, width) in enumerate(CHUNKS):
        rest = msg.at[pl.ds(0, nexp - 1), :, pl.ds(off, width)]
        pltpu.make_async_copy(rest, rest, a_send.at[c]).wait()

    for c, (off, width) in enumerate(BACK):
        d_own[c].wait()
        rest = recv_d.at[c, pl.ds(0, nexp - 1)]
        pltpu.make_async_copy(rest, rest, d_recv.at[c]).wait()
        got = recv_d[c].reshape(nexp * 16, WIDE)
        in_grad[:, pl.ds(off, WIDE)] = mm(upper, got).astype(BF16)
        if width > WIDE:
            in_grad[:, pl.ds(off + WIDE, WIDE)] = mm(lower, got).astype(BF16)

    for c in range(NBK):
        rest = msg_d.at[c, pl.ds(0, nexp - 1)]
        pltpu.make_async_copy(rest, rest, d_send.at[c]).wait()


def hand_on(grad_in, delta_in, grad_out, delta_out):
    grad_out[...] = grad_in[...]
    delta_out[...] = delta_in[...]


def on_device(
    nexp,
    ndp,
    tokens,
    out_grad,
    expert_ids,
    gate_weights,
    base_gate,
    base_up,
    base_down,
    block_ids,
    delta,
    moment_one,
    moment_two,
):
    vmem = pl.BlockSpec(memory_space=pltpu.VMEM)
    smem = pl.BlockSpec(memory_space=pltpu.SMEM)
    anym = pl.BlockSpec(memory_space=pl.ANY)
    dma = pltpu.SemaphoreType.DMA
    scratch = [
        pltpu.VMEM((TOP, TOK), jnp.int32),
        pltpu.VMEM((TOP, TOK), F32),
        pltpu.VMEM((TOK, FEAT), BF16),
        pltpu.VMEM((TOK, FEAT), BF16),
        pltpu.VMEM((nexp, 16, FEAT), BF16),
        pltpu.VMEM((nexp, 16, FEAT), BF16),
        pltpu.VMEM((FBLK, 2 * ROWS, BLK), BF16),
        pltpu.VMEM((D, 2 * HID), BF16),
        pltpu.VMEM((HID, D), BF16),
        pltpu.VMEM((2, 2, BLK, BLK), F32),
        pltpu.VMEM((2, 2, BLK, BLK), F32),
        pltpu.VMEM((2, 2, BLK, BLK), F32),
        pltpu.VMEM((6, BLK, BLK), F32),
        pltpu.VMEM((ROWS, 2 * HID), F32),
        pltpu.VMEM((ROWS, HID), F32),
        pltpu.VMEM((ROWS, 2 * HID), BF16),
        pltpu.VMEM((ROWS, HID), BF16),
        pltpu.VMEM((4, ROWS, FEAT), BF16),
        pltpu.VMEM((4, ROWS, FEAT), BF16),
        pltpu.VMEM((ROWS, FEAT), BF16),
        pltpu.VMEM((ROWS, FEAT), BF16),
        pltpu.VMEM((ROWS, FEAT), BF16),
        pltpu.VMEM((HALF, FEAT), F32),
        pltpu.VMEM((HALF, FEAT), F32),
        pltpu.VMEM((ROWS, FEAT), F32),
        pltpu.VMEM((HALF, FEAT), BF16),
        pltpu.VMEM((HALF, FEAT), BF16),
        pltpu.VMEM((ROWS, FEAT), BF16),
        pltpu.VMEM((ROWS, FEAT), BF16),
        pltpu.VMEM((NBK, nexp, 16, WIDE), BF16),
        pltpu.VMEM((NBK, nexp, 16, WIDE), BF16),
        dma((10,)),
        dma((NCH,)),
        dma((NCH,)),
        dma((NCH,)),
        dma((NCH, 13)),
        dma((NCH, 13)),
        dma((NSM, 4)),
        dma((NSM, 4)),
        dma((NSM, 6)),
        dma((NSM, 6)),
        dma((NBK,)),
        dma((NBK,)),
        dma((NBK,)),
    ]
    in_grad, new_delta = pl.pallas_call(
        functools.partial(kernel, nexp, ndp),
        out_shape=(
            jax.ShapeDtypeStruct((TOK, FEAT), BF16),
            jax.ShapeDtypeStruct((1, 2, 2, BLK, BLK), F32),
        ),
        in_specs=[anym, anym, smem] + [anym] * 8,
        out_specs=(vmem, vmem),
        scratch_shapes=scratch,
        compiler_params=pltpu.CompilerParams(
            collective_id=0, has_side_effects=True, vmem_limit_bytes=56 * 1024 * 1024
        ),
    )(
        expert_ids.T,
        gate_weights.T,
        block_ids,
        tokens,
        out_grad,
        base_gate,
        base_up,
        base_down,
        delta,
        moment_one,
        moment_two,
    )
    return pl.pallas_call(
        hand_on,
        out_shape=(
            jax.ShapeDtypeStruct(in_grad.shape, in_grad.dtype),
            jax.ShapeDtypeStruct(new_delta.shape, new_delta.dtype),
        ),
        in_specs=[vmem, vmem],
        out_specs=(vmem, vmem),
    )(in_grad, new_delta)


def solution(mesh):
    placed = (
        P("expert", None),
        P("expert", None),
        P("expert", None),
        P("expert", None),
        P("expert", None, "dp"),
        P("expert", None, "dp"),
        P("expert", "dp", None),
        P("expert", "dp", None),
        P("expert", "dp", None, None, None),
        P("expert", "dp", None, None, None),
        P("expert", "dp", None, None, None),
    )
    return jax.shard_map(
        functools.partial(on_device, mesh.shape["expert"], mesh.shape["dp"]),
        mesh=mesh,
        in_specs=placed,
        out_specs=(P("expert", "dp"), P("expert", "dp", None, None, None)),
        check_vma=False,
    )
```

```python
import functools

import jax
import jax.numpy as jnp
from jax import lax
from jax.experimental import pallas as pl
from jax.experimental.pallas import tpu as pltpu
from jax.sharding import PartitionSpec as P

D = 7168
FF = 2048
BLK = 128
CAP = 6
PAD = 8
TOK = 16
TOP = 8
HID = 256
ROWS = 192
HALF = ROWS // 2
FEAT = 896
FBLK = D // BLK
NT_DEV = FEAT // BLK


def cut(*widths):
    return tuple((sum(widths[:i]), w) for i, w in enumerate(widths))


CHUNKS = cut(256, 256, 384)
NCH = len(CHUNKS)
GROUPS = cut(256, 256, 384)
SUMS = cut(384, 256, 256)
NSM = len(SUMS)
BACK = cut(384, 256, 256)
NBK = len(BACK)
WIDE = tuple(128 if width <= 256 else 256 for _, width in BACK)
TAKE_KEYS = (0, 0.55, 0.7, 1.05, 1.2, 1.6, 1.75, 2.1)
GIVE_KEYS = (0, 0.5, 1.6, 2.7)

beta_one = 0.9
beta_two = 0.95
learn_rate = 0.5
adam_eps = 1e-08
corr_one = 1.0 - beta_one**10
corr_two = 1.0 - beta_two**10

MESH = pl.DeviceIdType.MESH
F32 = jnp.float32
BF16 = jnp.bfloat16
NT = (((1,), (1,)), ((), ()))
TN = (((0,), (0,)), ((), ()))


def last_of(parts, whole):
    ends = {off + width: (off, width) for off, width in whole}
    return {c: ends[off + width] for c, (off, width) in enumerate(parts) if off + width in ends}


def in_order(parts, keys):
    steps = [(c + key, c, step) for c in range(parts) for step, key in enumerate(keys)]
    return [step[1:] for step in sorted(steps)]


def mm(a, b):
    return jnp.dot(a, b, preferred_element_type=F32)


def mm_nt(a, b):
    return lax.dot_general(a, b, NT, preferred_element_type=F32)


def mm_tn(a, b):
    return lax.dot_general(a, b, TN, preferred_element_type=F32)


def slot_matrix(ids_t, gates_t, count, width_bits):
    place = lax.broadcasted_iota(jnp.int32, (count, TOK), 0)
    expert = place >> width_bits
    rank = (place & (PAD - 1)).astype(F32)
    named = jnp.zeros((count, TOK), F32)
    gates = jnp.zeros((count, TOK), F32)
    for k in range(TOP):
        hit = expert == ids_t[k : k + 1, :]
        named = jnp.where(hit, 1.0, named)
        gates = jnp.where(hit, gates_t[k : k + 1, :], gates)
    earlier = (
        lax.broadcasted_iota(jnp.int32, (TOK, TOK), 0)
        < lax.broadcasted_iota(jnp.int32, (TOK, TOK), 1)
    ).astype(F32)
    before = mm(named.astype(BF16), earlier.astype(BF16))
    chosen = jnp.where(before == rank, named, 0.0)
    return chosen, gates


def kernel(
    nexp,
    ndp,
    ids_hbm,
    gates_hbm,
    bids,
    tok_hbm,
    og_hbm,
    wg_hbm,
    wu_hbm,
    wd_hbm,
    delta_hbm,
    m1_hbm,
    m2_hbm,
    in_grad,
    new_delta,
    ids_v,
    gates_v,
    tok_v,
    og_v,
    msg,
    recv,
    gath,
    wgu,
    wd,
    delta_v,
    m1_v,
    m2_v,
    dz,
    gu_acc,
    hg_acc,
    gu_b,
    hid_b,
    p_send,
    p_recv,
    far_s,
    right_s,
    left_s,
    right_t,
    left_t,
    own_t,
    far_l,
    far_r,
    from_l,
    from_r,
    msg_d,
    recv_d,
    load_sem,
    a_send,
    a_recv,
    a_loc,
    g_send,
    g_recv,
    p_ssem,
    p_rsem,
    x_ssem,
    x_rsem,
    d_send,
    d_recv,
    d_loc,
):
    me_d = lax.axis_index("dp")
    me_e = lax.axis_index("expert")
    core = lax.rem(me_d, 2)
    flip = 1 - 2 * core
    partner = me_d + flip
    right = lax.rem(me_d + 2, ndp)
    left = lax.rem(me_d + ndp - 2, ndp)
    far = lax.rem(me_d + 4, ndp)

    barrier = pltpu.get_barrier_semaphore()

    def greet(i, carry):
        pl.semaphore_signal(
            barrier, inc=1, device_id={"expert": lax.rem(me_e + i, nexp)}, device_id_type=MESH
        )
        return carry

    lax.fori_loop(1, nexp, greet, 0)
    for other in (partner, right, left):
        pl.semaphore_signal(barrier, inc=1, device_id={"dp": other}, device_id_type=MESH)

    first = pl.multiple_of(me_d * FEAT, BLK)
    loads = [
        pltpu.make_async_copy(tok_hbm.at[:, pl.ds(first, FEAT)], tok_v, load_sem.at[0]),
        pltpu.make_async_copy(og_hbm.at[:, pl.ds(first, FEAT)], og_v, load_sem.at[1]),
        pltpu.make_async_copy(delta_hbm.at[0], delta_v, load_sem.at[2]),
        pltpu.make_async_copy(wg_hbm.at[0], wgu.at[:, pl.ds(0, HID)], load_sem.at[3]),
        pltpu.make_async_copy(wu_hbm.at[0], wgu.at[:, pl.ds(HID, HID)], load_sem.at[4]),
        pltpu.make_async_copy(wd_hbm.at[0], wd, load_sem.at[5]),
        pltpu.make_async_copy(m1_hbm.at[0], m1_v, load_sem.at[6]),
        pltpu.make_async_copy(m2_hbm.at[0], m2_v, load_sem.at[7]),
    ]
    tables = [
        pltpu.make_async_copy(ids_hbm, ids_v, load_sem.at[8]),
        pltpu.make_async_copy(gates_hbm, gates_v, load_sem.at[9]),
    ]
    for load in tables + loads:
        load.start()

    for load in tables:
        load.wait()
    ids_t = ids_v[...]
    gates_t = gates_v[...]
    chosen, gates = slot_matrix(ids_t, gates_t, nexp * PAD, 3)
    gate_of = jnp.sum(chosen * gates, axis=1, keepdims=True)
    chosen_b = chosen.astype(BF16)
    loads[0].wait()
    loads[1].wait()
    def build(c):
        off, width = CHUNKS[c]
        cols = pl.ds(off, width)
        rows_out = mm(chosen_b, tok_v[:, cols])
        grads_out = mm(chosen_b, og_v[:, cols]) * gate_of
        msg[:, :, cols] = jnp.concatenate(
            [rows_out.reshape(nexp, PAD, width), grads_out.reshape(nexp, PAD, width)], axis=1
        ).astype(BF16)

    build(0)

    pl.semaphore_wait(barrier, nexp - 1 + 3)

    a_own = []
    for c, (off, width) in enumerate(CHUNKS):
        cols = pl.ds(off, width)

        def send(i, carry, c=c, cols=cols):
            to = lax.rem(me_e + i, nexp)
            pltpu.make_async_remote_copy(
                src_ref=msg.at[to, :, cols],
                dst_ref=recv.at[me_e, :, cols],
                send_sem=a_send.at[c],
                recv_sem=a_recv.at[c],
                device_id={"expert": to},
                device_id_type=MESH,
            ).start()
            return carry

        if c > 0:
            build(c)
        lax.fori_loop(1, nexp, send, 0)
        own = pltpu.make_async_copy(msg.at[me_e, :, cols], recv.at[me_e, :, cols], a_loc.at[c])
        own.start()
        a_own.append(own)

    def adjust_all():
        loads[2].wait()
        for c in range(2):
            for m in range(2):
                scale = jnp.where(bids[0, c, m] >= 2 * FBLK, FF**-0.5, D**-0.5).astype(F32)
                dz[3 * c + m] = delta_v[c, m] * scale
            dz[3 * c + 2] = jnp.zeros((BLK, BLK), F32)
        for i in (3, 4, 5):
            loads[i].wait()

        def which(c, want):
            return 3 * c + jnp.where(bids[0, c, 0] == want, 0, jnp.where(bids[0, c, 1] == want, 1, 2))

        def adjust(j, carry):
            at = pl.ds(pl.multiple_of(j * BLK, BLK), BLK)
            for kind in range(2):
                for c in range(2):
                    lanes = pl.ds(kind * HID + c * BLK, BLK)
                    old = wgu[at, lanes].astype(F32)
                    wgu[at, lanes] = (old + dz[which(c, kind * FBLK + j)]).astype(BF16)
            for c in range(2):
                subl = pl.ds(c * BLK, BLK)
                old = wd[subl, at].astype(F32)
                wd[subl, at] = (old + dz[which(c, 2 * FBLK + j)]).astype(BF16)
            return carry

        lax.fori_loop(0, FBLK, adjust, 0)

    adjust_all()

    chosen_d, _ = slot_matrix(ids_t, gates_t, nexp * 16, 4)
    place = lax.broadcasted_iota(jnp.int32, (nexp * 16, TOK), 0) & PAD
    upper = jnp.where(place == 0, chosen_d, 0.0).T.astype(BF16)
    lower = jnp.where(place == 0, 0.0, chosen_d).T.astype(BF16)

    gu_acc[...] = jnp.zeros_like(gu_acc)
    hg_acc[...] = jnp.zeros_like(hg_acc)

    row_i = lax.broadcasted_iota(jnp.int32, (2 * ROWS, nexp * 16), 0)
    col_i = lax.broadcasted_iota(jnp.int32, (2 * ROWS, nexp * 16), 1)
    col_r = col_i & (PAD - 1)
    want = (col_i >> 4) * CAP + col_r + jnp.where((col_i & PAD) != 0, ROWS, 0)
    compact = jnp.where((row_i == want) & (col_r < CAP), 1.0, 0.0).astype(BF16)

    def other(d):
        return d + flip

    both = pl.ds(0, 2 * ROWS)
    rows_s = pl.ds(0, ROWS)
    grads_s = pl.ds(ROWS, ROWS)

    def part(c, idx, d, which_rows, to):
        off, width = CHUNKS[c]
        ref = gath.at[pl.ds(d * NT_DEV + off // BLK, width // BLK), which_rows, :]
        return pltpu.make_async_remote_copy(
            src_ref=ref,
            dst_ref=ref,
            send_sem=g_send.at[c, idx],
            recv_sem=g_recv.at[c, idx],
            device_id={"dp": to},
            device_id_type=MESH,
        )

    sent = []

    def go(copy):
        copy.start()
        sent.append(copy)

    def held(off, width, d, which_rows):
        at = d * NT_DEV + off // BLK
        return jnp.concatenate([gath[at + t, which_rows] for t in range(width // BLK)], axis=1)

    group_of = last_of(CHUNKS, GROUPS)

    def use_rows(c, d):
        if c in group_of:
            off, width = group_of[c]
            at = pl.ds(pl.multiple_of(d * FEAT + off, BLK), width)
            gu_acc[...] += mm(held(off, width, d, rows_s), wgu[at, :])

    def use_grads(c, d):
        if c in group_of:
            off, width = group_of[c]
            at = pl.ds(pl.multiple_of(d * FEAT + off, BLK), width)
            hg_acc[...] += mm_nt(held(off, width, d, grads_s), wd[:, at])

    def take_own(c):
        off, width = CHUNKS[c]
        cols = pl.ds(off, width)
        a_own[c].wait()
        rest = recv.at[pl.ds(0, nexp - 1), :, cols]
        pltpu.make_async_copy(rest, rest, a_recv.at[c]).wait()
        got = recv[:, :, cols].reshape(nexp * 16, width)
        packed = mm(compact, got).astype(BF16)
        for t in range(width // BLK):
            gath[me_d * NT_DEV + off // BLK + t] = packed[:, t * BLK : (t + 1) * BLK]
        go(part(c, 0, me_d, rows_s, right))
        go(part(c, 1, me_d, grads_s, left))
        go(part(c, 2, me_d, grads_s, right))
        go(part(c, 3, me_d, rows_s, left))
        go(part(c, 6, me_d, both, partner))
        use_rows(c, me_d)
        use_grads(c, me_d)

    def take_near_first(c):
        part(c, 0, left, rows_s, me_d).wait_recv()
        go(part(c, 4, left, rows_s, right))
        go(part(c, 7, left, rows_s, partner))
        part(c, 1, right, grads_s, me_d).wait_recv()
        go(part(c, 5, right, grads_s, left))
        go(part(c, 8, right, grads_s, partner))
        use_rows(c, left)
        use_grads(c, right)

    def take_partner(c):
        part(c, 6, partner, both, me_d).wait_recv()
        use_rows(c, partner)
        use_grads(c, partner)

    def take_near_second(c):
        part(c, 2, left, grads_s, me_d).wait_recv()
        go(part(c, 9, left, grads_s, partner))
        part(c, 3, right, rows_s, me_d).wait_recv()
        go(part(c, 10, right, rows_s, partner))
        use_grads(c, left)
        use_rows(c, right)

    def take_passed_first(c):
        part(c, 7, other(left), rows_s, me_d).wait_recv()
        part(c, 8, other(right), grads_s, me_d).wait_recv()
        use_rows(c, other(left))
        use_grads(c, other(right))

    def take_far(c):
        part(c, 4, far, rows_s, me_d).wait_recv()
        go(part(c, 11, far, rows_s, partner))
        part(c, 5, far, grads_s, me_d).wait_recv()
        go(part(c, 12, far, grads_s, partner))
        use_rows(c, far)
        use_grads(c, far)

    def take_passed_second(c):
        part(c, 9, other(left), grads_s, me_d).wait_recv()
        part(c, 10, other(right), rows_s, me_d).wait_recv()
        use_grads(c, other(left))
        use_rows(c, other(right))

    def take_passed_far(c):
        part(c, 11, other(far), rows_s, me_d).wait_recv()
        use_rows(c, other(far))
        part(c, 12, other(far), grads_s, me_d).wait_recv()
        use_grads(c, other(far))

    takes = (
        take_own,
        take_near_first,
        take_partner,
        take_near_second,
        take_passed_first,
        take_far,
        take_passed_second,
        take_passed_far,
    )
    for c, step in in_order(NCH, TAKE_KEYS):
        takes[step](c)

    gate_pre = gu_acc[:, :HID]
    up_pre = gu_acc[:, HID:]
    hidden_grad = hg_acc[...]
    sig = jax.nn.sigmoid(gate_pre)
    swish = gate_pre * sig
    hid_b[...] = (swish * up_pre).astype(BF16)
    gu_b[:, :HID] = (hidden_grad * up_pre * sig * (1.0 + gate_pre * (1.0 - sig))).astype(BF16)
    gu_b[:, HID:] = (hidden_grad * swish).astype(BF16)

    targets = (far, right, left, me_d)

    def term(c, d):
        off, width = SUMS[c]
        at = pl.ds(pl.multiple_of(d * FEAT + off, BLK), width)
        return mm_nt(gu_b[...], wgu[at, :])

    def pair(c, j):
        cols = pl.ds(*SUMS[c])
        return pltpu.make_async_remote_copy(
            src_ref=p_send.at[j, :, cols],
            dst_ref=p_recv.at[j, :, cols],
            send_sem=p_ssem.at[c, j],
            recv_sem=p_rsem.at[c, j],
            device_id={"dp": partner},
            device_id_type=MESH,
        )

    def ring(c, idx, src, dst, to):
        return pltpu.make_async_remote_copy(
            src_ref=src,
            dst_ref=dst,
            send_sem=x_ssem.at[c, idx],
            recv_sem=x_rsem.at[c, idx],
            device_id={"dp": to},
            device_id_type=MESH,
        )

    low = pl.ds(0, HALF)
    high = pl.ds(HALF, HALF)

    def ring_copies(c):
        cols = pl.ds(*SUMS[c])
        return (
            ring(c, 0, far_s.at[low, cols], far_l.at[:, cols], right),
            ring(c, 1, far_s.at[high, cols], far_r.at[:, cols], left),
            ring(c, 2, right_s.at[high, cols], from_l.at[high, cols], right),
            ring(c, 3, left_s.at[low, cols], from_r.at[low, cols], left),
            ring(c, 4, right_s.at[low, cols], from_l.at[low, cols], right),
            ring(c, 5, left_s.at[high, cols], from_r.at[high, cols], left),
        )

    def give_partner(c, j):
        cols = pl.ds(*SUMS[c])
        p_send[j, :, cols] = term(c, other(targets[j])).astype(BF16)
        go(pair(c, j))

    def summed(c, j):
        cols = pl.ds(*SUMS[c])
        value = term(c, targets[j])
        pair(c, j).wait_recv()
        return value + p_recv[j, :, cols].astype(F32)

    def ring_first(c):
        cols = pl.ds(*SUMS[c])
        copies = ring_copies(c)
        far_s[:, cols] = summed(c, 0).astype(BF16)
        go(copies[0])
        go(copies[1])
        value = summed(c, 1)
        right_s[high, cols] = value[HALF:].astype(BF16)
        go(copies[2])
        right_t[:, cols] = value[:HALF]
        value = summed(c, 2)
        left_s[low, cols] = value[:HALF].astype(BF16)
        go(copies[3])
        left_t[:, cols] = value[HALF:]

    def ring_second(c):
        cols = pl.ds(*SUMS[c])
        copies = ring_copies(c)
        copies[0].wait_recv()
        right_s[low, cols] = (right_t[:, cols] + far_l[:, cols].astype(F32)).astype(BF16)
        go(copies[4])
        copies[1].wait_recv()
        left_s[high, cols] = (left_t[:, cols] + far_r[:, cols].astype(F32)).astype(BF16)
        go(copies[5])
        own_t[:, cols] = summed(c, 3)

    back_row = lax.broadcasted_iota(jnp.int32, (nexp * PAD, ROWS), 0)
    back_col = lax.broadcasted_iota(jnp.int32, (nexp * PAD, ROWS), 1)
    back_r = back_row & (PAD - 1)
    spread = jnp.where(
        (back_col == (back_row >> 3) * CAP + back_r) & (back_r < CAP), 1.0, 0.0
    ).astype(BF16)
    d_own = []

    def give_back(c):
        off, width = BACK[c]
        cols = pl.ds(off, width)
        for p, (low_end, size) in enumerate(SUMS):
            if off <= low_end < off + width:
                for copy in ring_copies(p)[2:]:
                    copy.wait_recv()
        total = own_t[:, cols] + from_l[:, cols].astype(F32) + from_r[:, cols].astype(F32)
        wide = mm(spread, total.astype(BF16)).reshape(nexp, PAD, width)
        half = WIDE[c]
        second = wide[:, :, half:]
        if width < 2 * half:
            blank = jnp.zeros((nexp, PAD, 2 * half - width), F32)
            second = blank if width == half else jnp.concatenate([second, blank], axis=2)
        msg_d[c, :, :, :half] = jnp.concatenate([wide[:, :, :half], second], axis=1).astype(BF16)

        def send(i, carry):
            to = lax.rem(me_e + i, nexp)
            pltpu.make_async_remote_copy(
                src_ref=msg_d.at[c, to, :, pl.ds(0, WIDE[c])],
                dst_ref=recv_d.at[c, me_e, :, pl.ds(0, WIDE[c])],
                send_sem=d_send.at[c],
                recv_sem=d_recv.at[c],
                device_id={"expert": to},
                device_id_type=MESH,
            ).start()
            return carry

        lax.fori_loop(1, nexp, send, 0)
        cells = pl.ds(0, WIDE[c])
        own = pltpu.make_async_copy(
            msg_d.at[c, me_e, :, cells], recv_d.at[c, me_e, :, cells], d_loc.at[c]
        )
        own.start()
        d_own.append(own)

    def give_partner_all(c):
        for j in range(4):
            give_partner(c, j)

    ends = last_of(SUMS, BACK)

    def finish(c):
        if c in ends:
            give_back(BACK.index(ends[c]))

    gives = (give_partner_all, ring_first, ring_second, finish)
    for c, step in in_order(NSM, GIVE_KEYS):
        gives[step](c)

    loads[6].wait()
    loads[7].wait()
    for c in range(2):
        lanes = pl.ds(c * BLK, BLK)
        h_part = hid_b[:, lanes]
        g_part = gu_b[:, lanes]
        u_part = gu_b[:, pl.ds(HID + c * BLK, BLK)]
        for m in range(2):
            ident = bids[0, c, m]
            kind = jnp.where(ident >= 2 * FBLK, 2, jnp.where(ident >= FBLK, 1, 0))
            rows_both = gath[ident - kind * FBLK]
            x_part = rows_both[:ROWS]
            y_part = rows_both[ROWS:]
            lhs = jnp.where(kind == 2, h_part, x_part)
            rhs = jnp.where(kind == 0, g_part, jnp.where(kind == 1, u_part, y_part))
            scale = jnp.where(kind == 2, FF**-0.5, D**-0.5).astype(F32)
            grad = mm_tn(lhs, rhs) * scale
            mom_one = beta_one * m1_v[c, m] + (1.0 - beta_one) * grad
            mom_two = beta_two * m2_v[c, m] + (1.0 - beta_two) * grad * grad
            new_delta[0, c, m] = delta_v[c, m] - learn_rate * (mom_one / corr_one) / (
                jnp.sqrt(mom_two / corr_two) + adam_eps
            )

    for copy in sent:
        copy.wait_send()
    for c, (off, width) in enumerate(CHUNKS):
        rest = msg.at[pl.ds(0, nexp - 1), :, pl.ds(off, width)]
        pltpu.make_async_copy(rest, rest, a_send.at[c]).wait()

    for c, (off, width) in enumerate(BACK):
        d_own[c].wait()
        half = WIDE[c]
        rest = recv_d.at[c, pl.ds(0, nexp - 1), :, pl.ds(0, half)]
        pltpu.make_async_copy(rest, rest, d_recv.at[c]).wait()
        got = recv_d[c, :, :, :half].reshape(nexp * 16, half)
        in_grad[:, pl.ds(off, half)] = mm(upper, got).astype(BF16)
        tail = width - half
        if tail > 0:
            in_grad[:, pl.ds(off + half, tail)] = mm(lower, got[:, :tail]).astype(BF16)

    for c in range(NBK):
        rest = msg_d.at[c, pl.ds(0, nexp - 1), :, pl.ds(0, WIDE[c])]
        pltpu.make_async_copy(rest, rest, d_send.at[c]).wait()


def hand_on(grad_in, delta_in, grad_out, delta_out):
    grad_out[...] = grad_in[...]
    delta_out[...] = delta_in[...]


def on_device(
    nexp,
    ndp,
    tokens,
    out_grad,
    expert_ids,
    gate_weights,
    base_gate,
    base_up,
    base_down,
    block_ids,
    delta,
    moment_one,
    moment_two,
):
    vmem = pl.BlockSpec(memory_space=pltpu.VMEM)
    smem = pl.BlockSpec(memory_space=pltpu.SMEM)
    anym = pl.BlockSpec(memory_space=pl.ANY)
    dma = pltpu.SemaphoreType.DMA
    scratch = [
        pltpu.VMEM((TOP, TOK), jnp.int32),
        pltpu.VMEM((TOP, TOK), F32),
        pltpu.VMEM((TOK, FEAT), BF16),
        pltpu.VMEM((TOK, FEAT), BF16),
        pltpu.VMEM((nexp, 16, FEAT), BF16),
        pltpu.VMEM((nexp, 16, FEAT), BF16),
        pltpu.VMEM((FBLK, 2 * ROWS, BLK), BF16),
        pltpu.VMEM((D, 2 * HID), BF16),
        pltpu.VMEM((HID, D), BF16),
        pltpu.VMEM((2, 2, BLK, BLK), F32),
        pltpu.VMEM((2, 2, BLK, BLK), F32),
        pltpu.VMEM((2, 2, BLK, BLK), F32),
        pltpu.VMEM((6, BLK, BLK), F32),
        pltpu.VMEM((ROWS, 2 * HID), F32),
        pltpu.VMEM((ROWS, HID), F32),
        pltpu.VMEM((ROWS, 2 * HID), BF16),
        pltpu.VMEM((ROWS, HID), BF16),
        pltpu.VMEM((4, ROWS, FEAT), BF16),
        pltpu.VMEM((4, ROWS, FEAT), BF16),
        pltpu.VMEM((ROWS, FEAT), BF16),
        pltpu.VMEM((ROWS, FEAT), BF16),
        pltpu.VMEM((ROWS, FEAT), BF16),
        pltpu.VMEM((HALF, FEAT), F32),
        pltpu.VMEM((HALF, FEAT), F32),
        pltpu.VMEM((ROWS, FEAT), F32),
        pltpu.VMEM((HALF, FEAT), BF16),
        pltpu.VMEM((HALF, FEAT), BF16),
        pltpu.VMEM((ROWS, FEAT), BF16),
        pltpu.VMEM((ROWS, FEAT), BF16),
        pltpu.VMEM((NBK, nexp, 16, max(WIDE)), BF16),
        pltpu.VMEM((NBK, nexp, 16, max(WIDE)), BF16),
        dma((10,)),
        dma((NCH,)),
        dma((NCH,)),
        dma((NCH,)),
        dma((NCH, 13)),
        dma((NCH, 13)),
        dma((NSM, 4)),
        dma((NSM, 4)),
        dma((NSM, 6)),
        dma((NSM, 6)),
        dma((NBK,)),
        dma((NBK,)),
        dma((NBK,)),
    ]
    in_grad, new_delta = pl.pallas_call(
        functools.partial(kernel, nexp, ndp),
        out_shape=(
            jax.ShapeDtypeStruct((TOK, FEAT), BF16),
            jax.ShapeDtypeStruct((1, 2, 2, BLK, BLK), F32),
        ),
        in_specs=[anym, anym, smem] + [anym] * 8,
        out_specs=(vmem, vmem),
        scratch_shapes=scratch,
        compiler_params=pltpu.CompilerParams(
            collective_id=0, has_side_effects=True, vmem_limit_bytes=56 * 1024 * 1024
        ),
    )(
        expert_ids.T,
        gate_weights.T,
        block_ids,
        tokens,
        out_grad,
        base_gate,
        base_up,
        base_down,
        delta,
        moment_one,
        moment_two,
    )
    return pl.pallas_call(
        hand_on,
        out_shape=(
            jax.ShapeDtypeStruct(in_grad.shape, in_grad.dtype),
            jax.ShapeDtypeStruct(new_delta.shape, new_delta.dtype),
        ),
        in_specs=[vmem, vmem],
        out_specs=(vmem, vmem),
    )(in_grad, new_delta)


def solution(mesh):
    placed = (
        P("expert", None),
        P("expert", None),
        P("expert", None),
        P("expert", None),
        P("expert", None, "dp"),
        P("expert", None, "dp"),
        P("expert", "dp", None),
        P("expert", "dp", None),
        P("expert", "dp", None, None, None),
        P("expert", "dp", None, None, None),
        P("expert", "dp", None, None, None),
    )
    return jax.shard_map(
        functools.partial(on_device, mesh.shape["expert"], mesh.shape["dp"]),
        mesh=mesh,
        in_specs=placed,
        out_specs=(P("expert", "dp"), P("expert", "dp", None, None, None)),
        check_vma=False,
    )
```
